32 devices in a mesh: seq: 4 (over x, core), chan: 8 (over z, y).
Axes of the slice: x: 2, y: 2, z: 4, core: 2. Of those that a mesh axis runs over, the one named last changes fastest.
Arguments:
- values: bfloat16 [1024, 4096], P('chan', 'seq'), may hold values from -6 to 6
- gate_acts: bfloat16 [1024, 4096], P('chan', 'seq'), may hold values from -6 to 6
- cotangent: bfloat16 [1024, 4096], P('chan', 'seq'), may hold values from -6 to 6
- filter_taps: float32 [1024, 4096], P('chan', 'seq'), may hold values from -160 to 160
- w_value: bfloat16 [1024, 1024], replicated, may hold values from -0.1875 to 0.1875
- w_gate: bfloat16 [1024, 1024], replicated, may hold values from -0.1875 to 0.1875
Outputs:
- input_grad: bfloat16 [4096, 1024], P(('seq', 'chan'))
- filter_grad: float32 [1024, 4096], P('chan', 'seq')
The draws below stay inside these ranges and needn't reach their ends.
All inputs are finite; a program needn't handle non-finite values.
Results may differ from the reference program's by a relative error of at most 0.005.
Values may be sent and summed in bfloat16 or wider, within the bound.
No kernel may reach another device: no remote copies, remote signals or barrier semaphores. Data moves between devices by JAX's collectives and lax.ppermute only.
A program may use at most 128 MiB of HBM per device.

```python
import math
import jax
import jax.numpy as jnp
from jax import lax

D = 1024
SEQ = 4096


def draw_filter_taps(key, part):
    keys = jax.random.split(key, 4)
    slow_share = 0.5
    chooser = jax.random.uniform(keys[0], (D, 1), jnp.float32)
    slow_rate = jnp.exp(jax.random.uniform(keys[1], (D, 1), jnp.float32, math.log(0.2 / SEQ), math.log(2.0 / SEQ)))
    fast_rate = jnp.exp(jax.random.uniform(keys[2], (D, 1), jnp.float32, math.log(1.0 / 50.0), math.log(1.0 / 30.0)))
    rate = jnp.where(chooser < slow_share, slow_rate, fast_rate)
    lags = jnp.arange(SEQ, dtype=jnp.float32)[None, :]
    envelope = jnp.exp(-rate * lags)
    energy = jnp.expm1(-2.0 * rate * SEQ) / jnp.expm1(-2.0 * rate)
    amplitude = jnp.sqrt(SEQ / energy)
    noise = jnp.clip(jax.random.normal(keys[3], (D, SEQ), jnp.float32), -4.0, 4.0)
    return jnp.clip(noise * envelope * amplitude, -160.0, 160.0).astype(jnp.float32)


def block_levels(key, shape, shards, low, largest):
    def one(dim, shards_of):
        heights = jax.random.uniform(jax.random.fold_in(jax.random.fold_in(key, 6), dim), (shards_of,), jnp.float32, low / len(shards), largest / len(shards))
        return jnp.repeat(jnp.exp(heights), shape[dim] // shards_of).reshape((-1,) + (1,) * (len(shape) - dim - 1))

    gain = one(*shards[0])
    for cut in shards[1:]:
        gain = gain * one(*cut)
    return gain


def normal_values(stream_key, extent, width, bound, cuts=(), kind=jnp.bfloat16):
    drawn = width * jax.random.normal(stream_key, extent, jnp.float32)
    if cuts:
        drawn = drawn * block_levels(stream_key, extent, cuts, -0.22, 0.18)
    return jnp.clip(drawn, -bound, bound).astype(kind)


def setup_inputs(seed: int = 0) -> dict:
    splits = jax.random.split(jax.random.key(seed), 7)
    return {
        "values": normal_values(splits[0], (D, SEQ), 1.0, 6.0, ((0, 8), (1, 4))),
        "gate_acts": normal_values(splits[1], (D, SEQ), 1.0, 6.0, ((0, 8), (1, 4))),
        "cotangent": normal_values(splits[2], (D, SEQ), 1.0, 6.0, ((0, 8), (1, 4))),
        "filter_taps": draw_filter_taps(jax.random.fold_in(splits[6], 71), 0),
        "w_value": normal_values(splits[4], (D, D), D ** -0.5, 0.1875),
        "w_gate": normal_values(splits[5], (D, D), D ** -0.5, 0.1875),
    }


def block_grads(blocks):
    values, gate_acts, cotangent, filter_taps = blocks
    length = 2 * SEQ
    factor = 1.0 / math.sqrt(SEQ)
    kernel = filter_taps.astype(jnp.float32) * factor
    signal = values.astype(jnp.float32)
    upstream = cotangent.astype(jnp.float32) * gate_acts.astype(jnp.float32)
    kernel_spec = jnp.fft.rfft(kernel, n=length, axis=-1)
    signal_spec = jnp.fft.rfft(signal, n=length, axis=-1)
    upstream_spec = jnp.fft.rfft(upstream, n=length, axis=-1)
    conv_out = jnp.fft.irfft(kernel_spec * signal_spec, n=length, axis=-1)[:, :SEQ]
    value_grad = jnp.fft.irfft(jnp.conj(kernel_spec) * upstream_spec, n=length, axis=-1)[:, :SEQ]
    taps_grad = jnp.fft.irfft(upstream_spec * jnp.conj(signal_spec), n=length, axis=-1)[:, :SEQ] * factor
    gate_grad = cotangent.astype(jnp.float32) * conv_out
    return (value_grad.astype(jnp.bfloat16), gate_grad.astype(jnp.bfloat16), taps_grad.astype(jnp.float32))

def reference(values, gate_acts, cotangent, filter_taps, w_value, w_gate):
    group_size = 64
    blocks_count = D // group_size

    def split_rows(array):
        return array.reshape(blocks_count, group_size, SEQ)
    value_grad, gate_grad, taps_grad = lax.map(block_grads, (split_rows(values), split_rows(gate_acts), split_rows(cotangent), split_rows(filter_taps)))
    value_grad = value_grad.reshape(D, SEQ)
    gate_grad = gate_grad.reshape(D, SEQ)
    input_grad = jnp.dot(value_grad.T, w_value.T, preferred_element_type=jnp.float32)
    input_grad = input_grad + jnp.dot(gate_grad.T, w_gate.T, preferred_element_type=jnp.float32)
    return (input_grad.astype(jnp.bfloat16), taps_grad.reshape(D, SEQ))
```

```python
import functools
import math

import jax
import jax.numpy as jnp
import numpy as np
from jax import lax
from jax.experimental import pallas as pl
from jax.experimental.pallas import tpu as pltpu
from jax.sharding import PartitionSpec as P

LANES = 128
VALUE, TAPS, COT, GATE = range(4)


def halves(table):
    high = table.astype(jnp.bfloat16)
    low = (table - high.astype(np.float64)).astype(jnp.bfloat16)
    return high, low


def dft_tables(total):
    outer = total // LANES
    k1 = np.arange(outer) + 0.25
    a = np.arange(outer)
    b = np.arange(LANES)
    first = np.exp(-2j * np.pi * np.outer(k1, a) / outer)
    first = np.concatenate([first.real, first.imag], 0)
    turn = np.exp(-2j * np.pi * np.outer(k1, b) / total)
    second = np.exp(-2j * np.pi * np.outer(b, b) / LANES)
    second = np.block([[second.real, second.imag], [-second.imag, second.real]])
    back_second = second.T / total / math.sqrt(total)
    back_first = np.exp(2j * np.pi * np.outer(a, k1) / outer)
    back_first = np.concatenate([back_first.real, -back_first.imag], 1)

    f_hi, f_lo = halves(first)
    s_hi, s_lo = halves(second)
    bs_hi, bs_lo = halves(back_second)
    bf_hi, bf_lo = halves(back_first)
    return (
        np.concatenate([f_hi, f_lo], 1),
        np.concatenate([f_hi, f_hi, f_lo], 1),
        np.concatenate([s_hi, s_hi, s_lo], 0),
        turn.real.astype(np.float32),
        turn.imag.astype(np.float32),
        np.concatenate([bs_hi, bs_hi, bs_lo], 0),
        np.concatenate([bf_hi, bf_hi, bf_lo], 1),
    )


def split_terms(x):
    high = x.astype(jnp.bfloat16)
    low = (x - high.astype(jnp.float32)).astype(jnp.bfloat16)
    return high, low


def dot(left, right):
    return jnp.dot(left, right, preferred_element_type=jnp.float32)


def wide_dot(x, table):
    high, low = split_terms(x)
    return dot(jnp.concatenate([high, low, high], 1), table)


def mixer_kernel(
    n_seq,
    group,
    *rest,
):
    blocks = rest[:n_seq]
    f2, f3, s3, turn_re, turn_im, bs3, bf3 = rest[n_seq : n_seq + 7]
    grads, taps_out = rest[n_seq + 7 : n_seq + 9]
    sig, taps, up, cot, grads32, taps32 = rest[n_seq + 9 :]
    me = lax.axis_index("seq")
    _, channels, seq_len = blocks[0].shape
    outer = sig.shape[0] // channels
    own_outer = seq_len // LANES

    for k in range(n_seq):
        source = lax.bitwise_xor(me, k)
        for part in range(own_outer):
            cols = pl.ds(part * LANES, LANES)
            v, f, c, g = (blocks[k][i, :, cols].astype(jnp.float32) for i in range(4))
            rows = pl.ds(source * own_outer + part, channels, stride=outer)
            sig[rows, :] = v
            taps[rows, :] = f
            up[rows, :] = c * g
            cot[rows, :] = c

    def some(step, carry):
        base = step * group
        tr, ti = turn_re[...], turn_im[...]

        def forward(ref, exact):
            turned = []
            for pair in range(group // 2):
                xs = [
                    ref[pl.ds(pl.multiple_of((base + 2 * pair + i) * outer, outer), outer), :]
                    for i in range(2)
                ]
                x = jnp.concatenate(xs, 1)
                if exact:
                    high = x.astype(jnp.bfloat16)
                    y = dot(f2[...], jnp.concatenate([high, high], 0))
                else:
                    high, low = split_terms(x)
                    y = dot(f3[...], jnp.concatenate([high, low, high], 0))
                for i in range(2):
                    re = y[:outer, i * LANES : (i + 1) * LANES]
                    im = y[outer:, i * LANES : (i + 1) * LANES]
                    turned.append(jnp.concatenate([re * tr - im * ti, re * ti + im * tr], 1))
            spec = wide_dot(jnp.concatenate(turned, 0), s3[...])
            return spec[:, :LANES], spec[:, LANES:]

        def backward(re, im):
            mid = wide_dot(jnp.concatenate([re, im], 1), bs3[...])
            for pair in range(group // 2):
                cols = []
                for i in range(2):
                    rows = slice((2 * pair + i) * outer, (2 * pair + i + 1) * outer)
                    re, im = mid[rows, :LANES], mid[rows, LANES:]
                    cols.append(jnp.concatenate([re * tr + im * ti, im * tr - re * ti], 0))
                high, low = split_terms(jnp.concatenate(cols, 1))
                y = dot(bf3[...], jnp.concatenate([high, low, high], 0))
                for i in range(2):
                    yield base + 2 * pair + i, y[:, i * LANES : (i + 1) * LANES]

        kr, ki = forward(taps, True)
        vr, vi = forward(sig, True)
        ur, ui = forward(up, False)
        for ch, y in backward(kr * vr - ki * vi, kr * vi + ki * vr):
            held = cot[pl.ds(pl.multiple_of(ch * outer, outer), outer), :]
            grads32[pl.ds(channels + ch, outer, stride=2 * channels), :] = y * held
        for ch, y in backward(kr * ur + ki * ui, kr * ui - ki * ur):
            grads32[pl.ds(ch, outer, stride=2 * channels), :] = y
        for ch, y in backward(ur * vr + ui * vi, ui * vr - ur * vi):
            taps32[pl.ds(ch, outer, stride=channels), :] = y
        return carry

    lax.fori_loop(0, channels // group, some, 0)

    for a in range(outer):
        grads[a] = grads32[a * 2 * channels : (a + 1) * 2 * channels, :].astype(jnp.bfloat16)
    for k in range(n_seq):
        source = lax.bitwise_xor(me, k)
        for part in range(own_outer):
            start = pl.multiple_of((source * own_outer + part) * channels, channels)
            taps_out[k, :, pl.ds(part * LANES, LANES)] = taps32[pl.ds(start, channels), :].astype(jnp.bfloat16)


def project_kernel(n_seq, n_chan, grads, w_value, w_gate, own_taps, *rest):
    taps_in = rest[: n_seq - 1]
    out, taps_out, held = rest[n_seq - 1 :]
    me = lax.axis_index("seq")
    share = own_taps.shape[1]
    for s in range(n_seq):
        for c in range(n_chan):
            for g in range(2):
                held[g, pl.ds((c * n_seq + s) * share, share), :] = grads[
                    s * n_chan + c, g * share : (g + 1) * share, :
                ].astype(held.dtype)
    sides = [held[g].astype(jnp.bfloat16) for g in range(2)]
    total = dot(w_value[...], sides[0]) + dot(w_gate[...], sides[1])
    out[...] = total.T.astype(jnp.bfloat16)
    for k in range(n_seq):
        got = own_taps[0] if k == 0 else taps_in[k - 1][...]
        taps_out[lax.bitwise_xor(me, k)] = got.astype(jnp.float32)


def local(n_seq, n_chan, values, gate_acts, cotangent, filter_taps, w_value, w_gate):
    rows, seq_len = values.shape
    total = seq_len * n_seq
    channels = rows // n_seq
    outer = total // LANES
    tokens = total // (n_seq * n_chan)
    group = min(8, channels)
    me = lax.axis_index("seq")
    vmem = pl.BlockSpec(memory_space=pltpu.VMEM)

    taps16 = filter_taps.astype(jnp.bfloat16)
    fields = (values, taps16, cotangent, gate_acts)

    def route(k):
        return [(i, i ^ k) for i in range(n_seq)]

    got = {}
    for k in reversed(range(n_seq)):
        start = (me ^ k) * channels
        block = jnp.stack([lax.dynamic_slice_in_dim(x, start, channels, 0) for x in fields])
        got[k] = lax.ppermute(block, "seq", route(k)) if k else block

    tables = [jnp.asarray(t) for t in dft_tables(total)]
    args = [*(got[k] for k in range(n_seq)), *tables]
    long = pltpu.VMEM((channels * outer, LANES), jnp.float32)
    grads, taps_blocks = pl.pallas_call(
        functools.partial(mixer_kernel, n_seq, group),
        out_shape=(
            jax.ShapeDtypeStruct((outer, 2 * channels, LANES), jnp.bfloat16),
            jax.ShapeDtypeStruct((n_seq, channels, seq_len), jnp.bfloat16),
        ),
        in_specs=[vmem] * len(args),
        out_specs=(vmem, vmem),
        scratch_shapes=[long] * 4 + [pltpu.VMEM((2 * channels * outer, LANES), jnp.float32), long],
        compiler_params=pltpu.CompilerParams(vmem_limit_bytes=48 * 2**20),
        name="mixer",
    )(*args)

    if tokens != LANES:
        grads = grads.reshape(outer, 2 * channels, LANES // tokens, tokens).transpose(0, 2, 1, 3)
        grads = grads.reshape(n_seq * n_chan, 2 * channels, tokens)
    spread = lax.all_to_all(grads, ("seq", "chan"), 0, 0, tiled=True)
    taps_got = [lax.ppermute(taps_blocks[k], "seq", route(k)) for k in range(1, n_seq)]

    features = w_value.shape[0]
    args = [spread, w_value, w_gate, taps_blocks, *taps_got]
    held = jnp.bfloat16 if channels % 16 == 0 else jnp.float32
    input_grad, taps_grad = pl.pallas_call(
        functools.partial(project_kernel, n_seq, n_chan),
        out_shape=(
            jax.ShapeDtypeStruct((tokens, features), jnp.bfloat16),
            jax.ShapeDtypeStruct((n_seq, channels, seq_len), jnp.float32),
        ),
        in_specs=[vmem] * len(args),
        out_specs=(vmem, vmem),
        scratch_shapes=[pltpu.VMEM((2, rows * n_chan, tokens), held)],
        compiler_params=pltpu.CompilerParams(vmem_limit_bytes=32 * 2**20),
        name="project",
    )(*args)
    return input_grad, taps_grad.reshape(rows, seq_len)


def solution(mesh):
    return jax.shard_map(
        functools.partial(local, mesh.shape["seq"], mesh.shape["chan"]),
        mesh=mesh,
        in_specs=(P("chan", "seq"), P("chan", "seq"), P("chan", "seq"), P("chan", "seq"), P(), P()),
        out_specs=(P(("seq", "chan"), None), P("chan", "seq")),
        check_vma=False,
    )
```

```python
import functools
import math

import jax
import jax.numpy as jnp
import numpy as np
from jax import lax
from jax.experimental import pallas as pl
from jax.experimental.pallas import tpu as pltpu
from jax.sharding import PartitionSpec as P

LANES = 128
VALUE, TAPS, COT, GATE = range(4)
CHUNKS = 2
ONE_SPREAD = True
SLABS = 8
KEPT = 3
PAD = 8


def halves(table):
    high = table.astype(jnp.bfloat16)
    low = (table - high.astype(np.float64)).astype(jnp.bfloat16)
    return high, low


def dft_tables(total):
    outer = total // LANES
    k1 = np.arange(outer) + 0.25
    a = np.arange(outer)
    b = np.arange(LANES)
    first = np.exp(-2j * np.pi * np.outer(k1, a) / outer)
    first = np.concatenate([first.real, first.imag], 0)
    turn = np.exp(-2j * np.pi * np.outer(k1, b) / total)
    second = np.exp(-2j * np.pi * np.outer(b, b) / LANES)
    second = np.block([[second.real, second.imag], [-second.imag, second.real]])
    back_second = second.T / total / math.sqrt(total)
    back_first = np.exp(2j * np.pi * np.outer(a, k1) / outer)
    back_first = np.concatenate([back_first.real, -back_first.imag], 1)

    f_hi, f_lo = halves(first)
    s_hi, s_lo = halves(second)
    bs_hi, bs_lo = halves(back_second)
    bf_hi, bf_lo = halves(back_first)
    return (
        np.concatenate([f_hi, f_lo], 1),
        np.concatenate([f_hi, f_hi, f_lo], 1),
        np.concatenate([s_hi, s_hi, s_lo], 0),
        turn.real.astype(np.float32),
        turn.imag.astype(np.float32),
        np.concatenate([bs_hi, bs_hi, bs_lo], 0),
        np.concatenate([bf_hi, bf_hi, bf_lo], 1),
    )


def split_terms(x):
    high = x.astype(jnp.bfloat16)
    low = (x - high.astype(jnp.float32)).astype(jnp.bfloat16)
    return high, low


def dot(left, right):
    return jnp.dot(left, right, preferred_element_type=jnp.float32)


def wide_dot(x, table):
    high, low = split_terms(x)
    return dot(jnp.concatenate([high, low, high], 1), table)


def prep_kernel(n_seq, n_tables, values, filter_taps, cotangent, gate_acts, *rest):
    tables, rest = rest[:n_tables], rest[n_tables:]
    outs, held, (wide, sems, table_sems) = rest[: -n_tables - 3], rest[-n_tables - 3 : -3], rest[-3:]
    me = lax.axis_index("seq")
    chunks = len(outs) // n_seq
    rows = outs[0].shape[1]
    fields = {VALUE: values, COT: cotangent, GATE: gate_acts}
    copies = []
    for chunk in range(chunks):
        for k in reversed(range(n_seq)):
            at = chunk * n_seq + k
            start = pl.multiple_of((lax.bitwise_xor(me, k) * chunks + chunk) * rows, rows)
            mine = pl.ds(start, rows)
            copies.append([pltpu.make_async_copy(filter_taps.at[mine, :], wide.at[at], sems.at[at, TAPS])])
            for field, ref in fields.items():
                copies[-1].append(pltpu.make_async_copy(ref.at[mine, :], outs[at].at[field], sems.at[at, field]))
            for copy in copies[-1]:
                copy.start()
    brought = [pltpu.make_async_copy(tables[i], held[i], table_sems.at[i]) for i in range(n_tables)]
    for copy in brought:
        copy.start()
    for chunk in range(chunks):
        for k in reversed(range(n_seq)):
            at = chunk * n_seq + k
            group = copies[chunk * n_seq + n_seq - 1 - k]
            group[0].wait()
            outs[at][TAPS] = wide[at].astype(jnp.bfloat16)
            for copy in group[1:]:
                copy.wait()
    for copy in brought:
        copy.wait()


def mixer_kernel(
    n_seq,
    group,
    last,
    n_before,
    *rest,
):
    blocks, rest = rest[:n_seq], rest[n_seq:]
    (f2, f3, s3, turn_re, turn_im, bs3, bf3), rest = rest[:7], rest[7:]
    if last:
        before, rest = rest[:n_before], rest[n_before:]
    else:
        before = ()
    grads, taps_out, sig, taps, up, cot, grads32, taps32 = rest
    me = lax.axis_index("seq")
    _, channels, seq_len = blocks[0].shape
    outer = sig.shape[0] // channels - PAD
    pitch, wide, narrow = outer + PAD, 2 * channels + PAD, channels + PAD
    own_outer = seq_len // LANES

    for k in range(n_seq):
        source = lax.bitwise_xor(me, k)
        for part in range(own_outer):
            cols = pl.ds(part * LANES, LANES)
            v, f, c, g = (blocks[k][i, :, cols].astype(jnp.float32) for i in range(4))
            rows = pl.ds(source * own_outer + part, channels, stride=pitch)
            sig[rows, :] = v
            taps[rows, :] = f
            up[rows, :] = c * g
            cot[rows, :] = c

    def some(step, carry):
        base = step * group
        tr, ti = turn_re[...], turn_im[...]

        def forward(ref, exact):
            turned = []
            for pair in range(group // 2):
                xs = [
                    ref[pl.ds(pl.multiple_of((base + 2 * pair + i) * pitch, PAD), outer), :]
                    for i in range(2)
                ]
                x = jnp.concatenate(xs, 1)
                if exact:
                    high = x.astype(jnp.bfloat16)
                    y = dot(f2[...], jnp.concatenate([high, high], 0))
                else:
                    high, low = split_terms(x)
                    y = dot(f3[...], jnp.concatenate([high, low, high], 0))
                for i in range(2):
                    re = y[:outer, i * LANES : (i + 1) * LANES]
                    im = y[outer:, i * LANES : (i + 1) * LANES]
                    turned.append(jnp.concatenate([re * tr - im * ti, re * ti + im * tr], 1))
            spec = wide_dot(jnp.concatenate(turned, 0), s3[...])
            return spec[:, :LANES], spec[:, LANES:]

        def backward(re, im):
            mid = wide_dot(jnp.concatenate([re, im], 1), bs3[...])
            for pair in range(group // 2):
                cols = []
                for i in range(2):
                    rows = slice((2 * pair + i) * outer, (2 * pair + i + 1) * outer)
                    re, im = mid[rows, :LANES], mid[rows, LANES:]
                    cols.append(jnp.concatenate([re * tr + im * ti, im * tr - re * ti], 0))
                high, low = split_terms(jnp.concatenate(cols, 1))
                y = dot(bf3[...], jnp.concatenate([high, low, high], 0))
                for i in range(2):
                    yield base + 2 * pair + i, y[:, i * LANES : (i + 1) * LANES]

        kr, ki = forward(taps, True)
        vr, vi = forward(sig, True)
        ur, ui = forward(up, False)
        for ch, y in backward(kr * vr - ki * vi, kr * vi + ki * vr):
            held = cot[pl.ds(pl.multiple_of(ch * pitch, PAD), outer), :]
            grads32[pl.ds(channels + ch, outer, stride=wide), :] = y * held
        for ch, y in backward(kr * ur + ki * ui, kr * ui - ki * ur):
            grads32[pl.ds(ch, outer, stride=wide), :] = y
        for ch, y in backward(ur * vr + ui * vi, ui * vr - ur * vi):
            taps32[pl.ds(ch, outer, stride=narrow), :] = y
        return carry

    lax.fori_loop(0, channels // group, some, 0)

    first = grads.shape[1] - 2 * channels
    for a in range(outer):
        if first:
            grads[a, :first, :] = before[0][a]
        grads[a, first:, :] = grads32[a * wide : a * wide + 2 * channels, :].astype(jnp.bfloat16)
    first = taps_out.shape[1] - channels
    for k in range(n_seq):
        source = lax.bitwise_xor(me, k)
        if first:
            taps_out[k, :first, :] = before[-1][k]
        for part in range(own_outer):
            start = (source * own_outer + part) * narrow
            start = pl.multiple_of(start, PAD) if narrow % PAD == 0 else start
            taps_out[k, first:, pl.ds(part * LANES, LANES)] = taps32[pl.ds(start, channels), :].astype(jnp.bfloat16)


def taps_kernel(n_seq, w_value, w_gate, *rest):
    taps_in, (out, w_held, sems) = rest[:n_seq], rest[n_seq:]
    me = lax.axis_index("seq")
    rows = w_value.shape[0]
    keep = w_held.shape[0] - rows
    copies = [
        pltpu.make_async_copy(w_value, w_held.at[:rows, :], sems.at[0]),
        pltpu.make_async_copy(w_gate.at[:keep, :], w_held.at[rows:, :], sems.at[1]),
    ]
    for copy in copies:
        copy.start()
    for k in range(n_seq):
        out[lax.bitwise_xor(me, k)] = taps_in[k][...].astype(jnp.float32)
    for copy in copies:
        copy.wait()


def project_kernel(n_seq, n_chan, n_spread, chunks, w_held, w_gate, *rest):
    spread, (out, held, gate_held, sems) = rest[:n_spread], rest[n_spread:]
    features = w_gate.shape[0]
    slab = features // SLABS
    copies = []
    for i in range(SLABS - KEPT):
        rows = pl.ds((KEPT + i) * slab, slab)
        copies.append(pltpu.make_async_copy(w_gate.at[rows, :], gate_held.at[pl.ds(i * slab, slab), :], sems.at[i]))
        copies[-1].start()
    per = chunks // n_spread
    share = spread[0].shape[1] // 2 // per
    for s in range(n_seq):
        for c in range(n_chan):
            for chunk in range(chunks):
                for g in range(2):
                    start = ((c * n_seq + s) * chunks + chunk) * share
                    at = (chunk % per * 2 + g) * share
                    piece = spread[chunk // per][s * n_chan + c, at : at + share, :]
                    held[g, pl.ds(start, share), :] = piece.astype(held.dtype)
    sides = [held[g].astype(jnp.bfloat16) for g in range(2)]
    split = KEPT * slab
    total = dot(w_held[:features, :], sides[0])
    out[:, :split] = (total[:split] + dot(w_held[features:, :], sides[1])).T.astype(jnp.bfloat16)
    for copy in copies:
        copy.wait()
    out[:, split:] = (total[split:] + dot(gate_held[...], sides[1])).T.astype(jnp.bfloat16)


def local(n_seq, n_chan, values, gate_acts, cotangent, filter_taps, w_value, w_gate):
    rows, seq_len = values.shape
    total = seq_len * n_seq
    channels = rows // n_seq
    outer = total // LANES
    tokens = total // (n_seq * n_chan)
    me = lax.axis_index("seq")
    vmem = pl.BlockSpec(memory_space=pltpu.VMEM)
    hbm = pl.BlockSpec(memory_space=pltpu.HBM)

    def like(x):
        return pltpu.VMEM(x.shape, x.dtype)

    def stay(x):
        return pltpu.with_memory_space_constraint(x, pltpu.HBM)

    def route(k):
        return [(i, i ^ k) for i in range(n_seq)]

    chunks = CHUNKS if channels % (16 * CHUNKS) == 0 else 1
    part = channels // chunks
    tables = [jnp.asarray(t) for t in dft_tables(total)]
    if part % 16 == 0:
        *sent, = pl.pallas_call(
            functools.partial(prep_kernel, n_seq, len(tables)),
            out_shape=[pltpu.VMEM((4, part, seq_len), jnp.bfloat16)] * (chunks * n_seq)
            + [like(t) for t in tables],
            in_specs=[hbm] * (4 + len(tables)),
            out_specs=[vmem] * (chunks * n_seq + len(tables)),
            scratch_shapes=[
                pltpu.VMEM((chunks * n_seq, part, seq_len), jnp.float32),
                pltpu.SemaphoreType.DMA((chunks * n_seq, 4)),
                pltpu.SemaphoreType.DMA((len(tables),)),
            ],
            compiler_params=pltpu.CompilerParams(vmem_limit_bytes=8 * 2**20),
            cost_estimate=pl.CostEstimate(flops=0, bytes_accessed=4 * 2**20, transcendentals=0),
            name="prep",
        )(*(stay(x) for x in (values, filter_taps, cotangent, gate_acts, *tables)))
        tables = sent[chunks * n_seq :]
    else:
        fields = (values, filter_taps.astype(jnp.bfloat16), cotangent, gate_acts)
        sent = [
            jnp.stack([lax.dynamic_slice_in_dim(x, (me ^ k) * channels, channels, 0) for x in fields])
            for k in range(n_seq)
        ]

    got = {}
    for chunk in range(chunks):
        for k in reversed(range(n_seq)):
            block = sent[chunk * n_seq + k]
            got[chunk, k] = lax.ppermute(block, "seq", route(k)) if k else block

    long = pltpu.VMEM((part * (outer + PAD), LANES), jnp.float32)
    spread, taps_block, before = [], None, []
    for chunk in range(chunks):
        last = chunk == chunks - 1
        args = [*(got[chunk, k] for k in range(n_seq)), *tables]
        if last:
            args += before
        outs = [
            jax.ShapeDtypeStruct((outer, 2 * part * (chunks if last and ONE_SPREAD else 1), LANES), jnp.bfloat16),
            jax.ShapeDtypeStruct((n_seq, part * (chunks if last else 1), seq_len), jnp.bfloat16),
        ]
        grads, taps_block = pl.pallas_call(
            functools.partial(mixer_kernel, n_seq, min(16, part), last, len(before)),
            out_shape=outs,
            in_specs=[vmem] * len(args),
            out_specs=[vmem] * len(outs),
            scratch_shapes=[long] * 4
            + [pltpu.VMEM((outer * (x * part + PAD), LANES), jnp.float32) for x in (2, 1)],
            compiler_params=pltpu.CompilerParams(vmem_limit_bytes=24 * 2**20),
            cost_estimate=pl.CostEstimate(flops=5 * 10**9, bytes_accessed=2 * 2**20, transcendentals=0),
            name="mixer",
        )(*args)
        before = [grads, taps_block] if ONE_SPREAD else [taps_block]
        if ONE_SPREAD and not last:
            continue
        if tokens != LANES:
            width = grads.shape[1]
            grads = grads.reshape(outer, width, LANES // tokens, tokens).transpose(0, 2, 1, 3)
            grads = grads.reshape(n_seq * n_chan, width, tokens)
        spread.append(lax.all_to_all(grads, ("seq", "chan"), 0, 0, tiled=True))

    taps_got = [lax.ppermute(taps_block[k], "seq", route(k)) if k else taps_block[0] for k in range(n_seq)]
    taps_grad, w_held = pl.pallas_call(
        functools.partial(taps_kernel, n_seq),
        out_shape=[
            jax.ShapeDtypeStruct((n_seq, channels, seq_len), jnp.float32),
            pltpu.VMEM((w_value.shape[0] * (SLABS + KEPT) // SLABS, w_value.shape[1]), w_value.dtype),
        ],
        in_specs=[hbm] * 2 + [vmem] * n_seq,
        out_specs=[vmem] * 2,
        scratch_shapes=[pltpu.SemaphoreType.DMA((2,))],
        compiler_params=pltpu.CompilerParams(vmem_limit_bytes=8 * 2**20),
        name="taps",
    )(stay(w_value), stay(w_gate), *taps_got)

    held = jnp.bfloat16 if part % 16 == 0 else jnp.float32
    args = [w_held, stay(w_gate), *spread]
    input_grad = pl.pallas_call(
        functools.partial(project_kernel, n_seq, n_chan, len(spread), chunks),
        out_shape=jax.ShapeDtypeStruct((tokens, w_value.shape[0]), jnp.bfloat16),
        in_specs=[vmem, hbm] + [vmem] * len(spread),
        out_specs=vmem,
        scratch_shapes=[
            pltpu.VMEM((2, rows * n_chan, tokens), held),
            pltpu.VMEM((w_gate.shape[0] * (SLABS - KEPT) // SLABS, w_gate.shape[1]), w_gate.dtype),
            pltpu.SemaphoreType.DMA((SLABS - KEPT,)),
        ],
        compiler_params=pltpu.CompilerParams(vmem_limit_bytes=16 * 2**20),
        name="project",
    )(*args)
    return input_grad, taps_grad.reshape(rows, seq_len)


def solution(mesh):
    return jax.shard_map(
        functools.partial(local, mesh.shape["seq"], mesh.shape["chan"]),
        mesh=mesh,
        in_specs=(P("chan", "seq"), P("chan", "seq"), P("chan", "seq"), P("chan", "seq"), P(), P()),
        out_specs=(P(("seq", "chan"), None), P("chan", "seq")),
        check_vma=False,
    )
```

```python
import functools
import math

import jax
import jax.numpy as jnp
import numpy as np
from jax import lax
from jax.experimental import pallas as pl
from jax.experimental.pallas import tpu as pltpu
from jax.sharding import Mesh
from jax.sharding import PartitionSpec as P

LANES = 128
VALUE, TAPS, COT, GATE = range(4)
SLABS = 8
KEPT = 3
PAD = 8


def halves(table):
    high = table.astype(jnp.bfloat16)
    low = (table - high.astype(np.float64)).astype(jnp.bfloat16)
    return high, low


def dft_tables(total):
    outer = total // LANES
    k1 = np.arange(outer) + 0.25
    a = np.arange(outer)
    b = np.arange(LANES)
    first = np.exp(-2j * np.pi * np.outer(k1, a) / outer)
    first = np.concatenate([first.real, first.imag], 0)
    turn = np.exp(-2j * np.pi * np.outer(k1, b) / total)
    second = np.exp(-2j * np.pi * np.outer(b, b) / LANES)
    second = np.block([[second.real, second.imag], [-second.imag, second.real]])
    back_second = second.T / total / math.sqrt(total)
    back_first = np.exp(2j * np.pi * np.outer(a, k1) / outer)
    back_first = np.concatenate([back_first.real, -back_first.imag], 1)

    f_hi, f_lo = halves(first)
    s_hi, s_lo = halves(second)
    bs_hi, bs_lo = halves(back_second)
    bf_hi, bf_lo = halves(back_first)
    return (
        np.concatenate([f_hi, f_lo], 1),
        np.concatenate([f_hi, f_hi, f_lo], 1),
        np.concatenate([s_hi, s_hi, s_lo], 0),
        turn.real.astype(np.float32),
        turn.imag.astype(np.float32),
        np.concatenate([bs_hi, bs_hi, bs_lo], 0),
        np.concatenate([bf_hi, bf_hi, bf_lo], 1),
    )


def split_terms(x):
    high = x.astype(jnp.bfloat16)
    low = (x - high.astype(jnp.float32)).astype(jnp.bfloat16)
    return high, low


def dot(left, right):
    return jnp.dot(left, right, preferred_element_type=jnp.float32)


def wide_dot(x, table):
    high, low = split_terms(x)
    return dot(jnp.concatenate([high, low, high], 1), table)


def prep_kernel(steps, n_tables, values, filter_taps, cotangent, gate_acts, *rest):
    tables, rest = rest[:n_tables], rest[n_tables:]
    (narrow, wide, sems, table_sems), rest = rest[-4:], rest[:-4]
    outs, held = rest[: len(rest) - n_tables], rest[len(rest) - n_tables :]
    me = lax.axis_index("seq")
    channels = wide.shape[1]
    fields = {VALUE: values, COT: cotangent, GATE: gate_acts}
    copies = []
    for at, k in enumerate(steps):
        mine = pl.ds(pl.multiple_of(lax.bitwise_xor(me, k) * channels, channels), channels)
        copies.append([pltpu.make_async_copy(filter_taps.at[mine, :], wide.at[at], sems.at[at, TAPS])])
        for i, ref in enumerate(fields.values()):
            copies[-1].append(pltpu.make_async_copy(ref.at[mine, :], narrow.at[at, i], sems.at[at, i + (i > 0)]))
        for copy in copies[-1]:
            copy.start()
    brought = [pltpu.make_async_copy(tables[i], held[i], table_sems.at[i]) for i in range(n_tables)]
    for copy in brought:
        copy.start()
    for at in range(len(steps)):
        for copy in copies[at]:
            copy.wait()
        blocks = [wide[at], *(narrow[at, i].astype(jnp.float32) for i in range(3))]
        for field, block in zip((TAPS, VALUE, COT, GATE), blocks):
            first = 0
            for out in outs[at :: len(steps)]:
                size = out.shape[1]
                out[field] = block[first : first + size].astype(jnp.bfloat16)
                first += size
    for copy in brought:
        copy.wait()


def mixer_kernel(
    n_seq,
    group,
    offset,
    places,
    *rest,
):
    blocks, rest = rest[:n_seq], rest[n_seq:]
    (f2, f3, s3, turn_re, turn_im, bs3, bf3), rest = rest[:7], rest[7:]
    before = ()
    if offset:
        before, rest = rest[1:2], rest[2:]
    grads, taps_out, sig, taps, up, cot, grads32, taps32, grads16, sem = rest
    me = lax.axis_index("seq")
    _, channels, seq_len = blocks[0].shape
    outer = sig.shape[0] // channels - PAD
    pitch, wide, narrow = outer + PAD, 2 * channels + PAD, channels + PAD
    own_outer = seq_len // LANES

    for k in range(n_seq):
        source = lax.bitwise_xor(me, k)
        for part in range(own_outer):
            cols = pl.ds(part * LANES, LANES)
            v, f, c, g = (blocks[k][i, :, cols].astype(jnp.float32) for i in range(4))
            rows = pl.ds(source * own_outer + part, channels, stride=pitch)
            sig[rows, :] = v
            taps[rows, :] = f
            up[rows, :] = c * g
            cot[rows, :] = c

    tr, ti = turn_re[...], turn_im[...]

    def forward(ref, exact, base, out):
        turned = []
        ys = []
        for pair in range(group // 2):
            xs = [ref[pl.ds((base + 2 * pair + i) * pitch, outer), :] for i in range(2)]
            x = jnp.concatenate(xs, 1)
            if exact:
                high = x.astype(jnp.bfloat16)
                ys.append(dot(f2[...], jnp.concatenate([high, high], 0)))
            else:
                high, low = split_terms(x)
                ys.append(dot(f3[...], jnp.concatenate([high, low, high], 0)))
        yield
        for y in ys:
            for i in range(2):
                re = y[:outer, i * LANES : (i + 1) * LANES]
                im = y[outer:, i * LANES : (i + 1) * LANES]
                turned.append(jnp.concatenate([re * tr - im * ti, re * ti + im * tr], 1))
        high, low = split_terms(jnp.concatenate(turned, 0))
        yield
        spec = dot(jnp.concatenate([high, low, high], 1), s3[...])
        out += [spec[:, :LANES], spec[:, LANES:]]
        yield

    def backward(left, right, conj, base, put):
        (ar, ai), (br, bi) = left, right
        if conj:
            product = jnp.concatenate([ar * br + ai * bi, ai * br - ar * bi], 1)
        else:
            product = jnp.concatenate([ar * br - ai * bi, ar * bi + ai * br], 1)
        high, low = split_terms(product)
        yield
        mid = dot(jnp.concatenate([high, low, high], 1), bs3[...])
        yield
        terms = []
        for pair in range(group // 2):
            cols = []
            for i in range(2):
                rows = slice((2 * pair + i) * outer, (2 * pair + i + 1) * outer)
                re, im = mid[rows, :LANES], mid[rows, LANES:]
                cols.append(jnp.concatenate([re * tr + im * ti, im * tr - re * ti], 0))
            terms.append(split_terms(jnp.concatenate(cols, 1)))
        yield
        ys = [dot(bf3[...], jnp.concatenate([high, low, high], 0)) for high, low in terms]
        yield
        for pair, y in enumerate(ys):
            for i in range(2):
                put(base + 2 * pair + i, y[:, i * LANES : (i + 1) * LANES])
        yield

    def put_gate(ch, y):
        held = cot[pl.ds(ch * pitch, outer), :]
        grads32[pl.ds(channels + ch, outer, stride=wide), :] = y * held

    def put_value(ch, y):
        grads32[pl.ds(ch, outer, stride=wide), :] = y

    def put_taps(ch, y):
        taps32[pl.ds(ch, outer, stride=narrow), :] = y

    tasks = []
    for base in range(0, channels, group):
        k, v, u = [], [], []
        tasks += [
            forward(taps, True, base, k),
            forward(sig, True, base, v),
            forward(up, False, base, u),
            backward(k, v, False, base, put_gate),
            backward(u, k, True, base, put_value),
            backward(u, v, True, base, put_taps),
        ]
    live = []
    while tasks or live:
        live = [task for task in live if next(task, StopIteration) is None]
        if tasks:
            live.append(tasks.pop(0))
            next(live[-1])

    copy = pltpu.make_async_copy(grads16, grads.at[:, pl.ds(2 * offset, 2 * channels), :], sem)

    def send():
        for a in range(outer):
            grads16[places[a]] = grads32[a * wide : a * wide + 2 * channels, :].astype(jnp.bfloat16)
        copy.start()

    send()
    for k in range(n_seq):
        source = lax.bitwise_xor(me, k)
        for part in range(own_outer):
            start = (source * own_outer + part) * narrow
            start = pl.multiple_of(start, PAD) if narrow % PAD == 0 else start
            cols = pl.ds(part * LANES, LANES)
            parts = [x[k, :, cols] for x in before] + [taps32[pl.ds(start, channels), :]]
            taps_out[k, :, cols] = jnp.concatenate(parts, 0).astype(taps_out.dtype)
    copy.wait()


def taps_kernel(n_seq, w_value, w_gate, *rest):
    taps_in, (out, w_held, sems) = rest[:n_seq], rest[n_seq:]
    me = lax.axis_index("seq")
    rows = w_value.shape[0]
    keep = w_held.shape[0] - rows
    copies = [
        pltpu.make_async_copy(w_value, w_held.at[:rows, :], sems.at[0]),
        pltpu.make_async_copy(w_gate.at[:keep, :], w_held.at[rows:, :], sems.at[1]),
    ]
    for copy in copies:
        copy.start()
    for k in range(n_seq):
        out[lax.bitwise_xor(me, k)] = taps_in[k][...].astype(jnp.float32)
    for copy in copies:
        copy.wait()


def project_kernel(n_seq, n_far, n_near, sizes, w_held, w_gate, spread, out, held, gate_held, sems):
    features = w_gate.shape[0]
    slab = features // SLABS
    copies = []
    for i in range(SLABS - KEPT):
        rows = pl.ds((KEPT + i) * slab, slab)
        copies.append(pltpu.make_async_copy(w_gate.at[rows, :], gate_held.at[pl.ds(i * slab, slab), :], sems.at[i]))
        copies[-1].start()
    share = sum(sizes)
    firsts = [sum(sizes[:i]) for i in range(len(sizes))]
    for source, (near, s, far) in enumerate(np.ndindex(n_near, n_seq, n_far)):
        block = spread[source].astype(jnp.float32)
        rows = pl.ds(((far * n_near + near) * n_seq + s) * share, share)
        for g in range(2):
            pieces = [block[2 * at + g * size : 2 * at + (g + 1) * size] for at, size in zip(firsts, sizes)]
            held[g, rows, :] = jnp.concatenate(pieces, 0).astype(held.dtype)
    sides = [held[g].astype(jnp.bfloat16) for g in range(2)]
    split = KEPT * slab
    total = dot(w_held[:features, :], sides[0])
    out[:, :split] = (total[:split] + dot(w_held[features:, :], sides[1])).T.astype(jnp.bfloat16)
    for copy in copies:
        copy.wait()
    out[:, split:] = (total[split:] + dot(gate_held[...], sides[1])).T.astype(jnp.bfloat16)


def local(n_seq, n_far, n_near, values, gate_acts, cotangent, filter_taps, w_value, w_gate):
    rows, seq_len = values.shape
    n_chan = n_far * n_near
    total = seq_len * n_seq
    channels = rows // n_seq
    outer = total // LANES
    tokens = total // (n_seq * n_chan)
    me = lax.axis_index("seq")
    vmem = pl.BlockSpec(memory_space=pltpu.VMEM)
    hbm = pl.BlockSpec(memory_space=pltpu.HBM)

    def like(x):
        return pltpu.VMEM(x.shape, x.dtype)

    def stay(x):
        return pltpu.with_memory_space_constraint(x, pltpu.HBM)

    def route(k):
        return [(i, i ^ k) for i in range(n_seq)]

    sizes = (channels // 2, channels // 2) if channels % 32 == 0 else (channels,)
    chunks = len(sizes)
    tables = [jnp.asarray(t) for t in dft_tables(total)]

    def prep(steps, tables):
        outs = [pltpu.VMEM((4, size, seq_len), jnp.bfloat16) for size in sizes for _ in steps]
        outs += [like(t) for t in tables]
        got = pl.pallas_call(
            functools.partial(prep_kernel, steps, len(tables)),
            out_shape=outs,
            in_specs=[hbm] * (4 + len(tables)),
            out_specs=[vmem] * len(outs),
            scratch_shapes=[
                pltpu.VMEM((len(steps), 3, channels, seq_len), jnp.bfloat16),
                pltpu.VMEM((len(steps), channels, seq_len), jnp.float32),
                pltpu.SemaphoreType.DMA((len(steps), 4)),
                pltpu.SemaphoreType.DMA((max(len(tables), 1),)),
            ],
            compiler_params=pltpu.CompilerParams(vmem_limit_bytes=8 * 2**20),
            cost_estimate=pl.CostEstimate(flops=0, bytes_accessed=4 * 2**20, transcendentals=0),
            name="prep",
        )(*(stay(x) for x in (values, filter_taps, cotangent, gate_acts, *tables)))
        for chunk in range(chunks):
            for at, k in enumerate(steps):
                sent[chunk, k] = got[chunk * len(steps) + at]
        return got[chunks * len(steps) :]

    sent, got = {}, {}
    if chunks > 1:
        far = tuple(reversed(range(2, n_seq)))
        prep(far, [])
        tables = prep((1, 0), tables)
    else:
        fields = (values, filter_taps.astype(jnp.bfloat16), cotangent, gate_acts)
        for k in range(n_seq):
            rows_k = [lax.dynamic_slice_in_dim(x, (me ^ k) * channels, channels, 0) for x in fields]
            sent[0, k] = jnp.stack(rows_k)
    for chunk in range(chunks):
        for k in reversed(range(n_seq)):
            block = sent[chunk, k]
            got[chunk, k] = lax.ppermute(block, "seq", route(k)) if k else block

    places = list(range(outer))
    if tokens == LANES:
        for s, far, near in np.ndindex(n_seq, n_far, n_near):
            places[(s * n_far + far) * n_near + near] = (near * n_seq + s) * n_far + far
    grads, taps_block, offset = None, None, 0
    for chunk, size in enumerate(sizes):
        args = [*(got[chunk, k] for k in range(n_seq)), *tables]
        specs = [vmem] * len(args)
        aliases = {}
        if chunk:
            aliases = {len(args): 0}
            args += [grads, taps_block]
            specs += [hbm, vmem]
        long = pltpu.VMEM((size * (outer + PAD), LANES), jnp.float32)
        kind = jnp.bfloat16 if chunk == chunks - 1 else jnp.float32
        grads, taps_block = pl.pallas_call(
            functools.partial(mixer_kernel, n_seq, size if size <= 24 else 8, offset, places),
            out_shape=[
                pltpu.HBM((outer, 2 * channels, LANES), jnp.bfloat16),
                pltpu.VMEM((n_seq, offset + size, seq_len), kind),
            ],
            in_specs=specs,
            out_specs=[hbm, vmem],
            input_output_aliases=aliases,
            scratch_shapes=[long] * 4
            + [pltpu.VMEM((outer * (x * size + PAD), LANES), jnp.float32) for x in (2, 1)]
            + [pltpu.VMEM((outer, 2 * size, LANES), jnp.bfloat16), pltpu.SemaphoreType.DMA],
            compiler_params=pltpu.CompilerParams(vmem_limit_bytes=24 * 2**20),
            cost_estimate=pl.CostEstimate(flops=5 * 10**9, bytes_accessed=2 * 2**20, transcendentals=0),
            name="mixer",
        )(*args)
        offset += size
    if tokens != LANES:
        grads = grads.reshape(outer, 2 * channels, LANES // tokens, tokens).transpose(0, 2, 1, 3)
        grads = grads.reshape(n_seq, n_far, n_near, 2 * channels, tokens).transpose(2, 0, 1, 3, 4)
        grads = grads.reshape(n_seq * n_chan, 2 * channels, tokens)
    spread = lax.all_to_all(grads, ("near", "seq", "far"), 0, 0, tiled=True)

    taps_got = [lax.ppermute(taps_block[k], "seq", route(k)) if k else taps_block[0] for k in range(n_seq)]
    taps_grad, w_held = pl.pallas_call(
        functools.partial(taps_kernel, n_seq),
        out_shape=[
            jax.ShapeDtypeStruct((n_seq, channels, seq_len), jnp.float32),
            pltpu.VMEM((w_value.shape[0] * (SLABS + KEPT) // SLABS, w_value.shape[1]), w_value.dtype),
        ],
        in_specs=[hbm] * 2 + [vmem] * n_seq,
        out_specs=[vmem] * 2,
        scratch_shapes=[pltpu.SemaphoreType.DMA((2,))],
        compiler_params=pltpu.CompilerParams(vmem_limit_bytes=8 * 2**20),
        name="taps",
    )(stay(w_value), stay(w_gate), *taps_got)

    held = jnp.bfloat16 if channels % 16 == 0 else jnp.float32
    args = [w_held, stay(w_gate), spread]
    input_grad = pl.pallas_call(
        functools.partial(project_kernel, n_seq, n_far, n_near, sizes),
        out_shape=jax.ShapeDtypeStruct((tokens, w_value.shape[0]), jnp.bfloat16),
        in_specs=[vmem, hbm, vmem],
        out_specs=vmem,
        scratch_shapes=[
            pltpu.VMEM((2, rows * n_chan, tokens), held),
            pltpu.VMEM((w_gate.shape[0] * (SLABS - KEPT) // SLABS, w_gate.shape[1]), w_gate.dtype),
            pltpu.SemaphoreType.DMA((SLABS - KEPT,)),
        ],
        compiler_params=pltpu.CompilerParams(vmem_limit_bytes=16 * 2**20),
        name="project",
    )(*args)
    return input_grad, taps_grad.reshape(rows, seq_len)


def solution(mesh):
    n_seq, n_chan = mesh.shape["seq"], mesh.shape["chan"]
    n_far = math.gcd(n_chan, 4)
    parts = Mesh(mesh.devices.reshape(n_seq, n_far, n_chan // n_far), ("seq", "far", "near"))
    chan = ("far", "near")
    return jax.shard_map(
        functools.partial(local, n_seq, n_far, n_chan // n_far),
        mesh=parts,
        in_specs=(P(chan, "seq"), P(chan, "seq"), P(chan, "seq"), P(chan, "seq"), P(), P()),
        out_specs=(P(("seq", *chan), None), P(chan, "seq")),
        check_vma=False,
    )
```

```python
import functools
import math

import jax
import jax.numpy as jnp
import numpy as np
from jax import lax
from jax.experimental import pallas as pl
from jax.experimental.pallas import tpu as pltpu
from jax.sharding import Mesh
from jax.sharding import PartitionSpec as P

LANES = 128
VALUE, TAPS, COT, GATE = range(4)
SLABS = 8
KEPT = 3
PAD = 8


def halves(table):
    high = table.astype(jnp.bfloat16)
    low = (table - high.astype(np.float64)).astype(jnp.bfloat16)
    return high, low


def dft_tables(total, n_seq):
    outer = total // LANES
    k1 = np.arange(outer) + 0.25
    a = np.arange(outer)
    b = np.arange(LANES)
    first = np.exp(-2j * np.pi * np.outer(k1, a) / outer)
    first = np.concatenate([first.real, first.imag], 0)
    turn = np.exp(-2j * np.pi * np.outer(k1, b) / total)
    second = np.exp(-2j * np.pi * np.outer(b, b) / LANES)
    second = np.block([[second.real, second.imag], [-second.imag, second.real]])
    back_second = second.T / total / math.sqrt(total)
    back_first = np.exp(2j * np.pi * np.outer(a, k1) / outer)
    back_first = np.concatenate([back_first.real, -back_first.imag], 1)

    parts = first.reshape(2 * outer, n_seq, outer // n_seq)
    orders = np.arange(n_seq)[:, None] ^ np.arange(n_seq)
    first = np.stack([parts[:, order].reshape(2 * outer, outer) for order in orders])
    f_hi, f_lo = halves(first)
    s_hi, s_lo = halves(second)
    bs_hi, bs_lo = halves(back_second)
    bf_hi, bf_lo = halves(back_first)
    return (
        np.concatenate([f_hi, f_lo], 2),
        np.concatenate([f_hi, f_hi, f_lo], 2),
        np.concatenate([s_hi, s_hi, s_lo], 0),
        turn.real.astype(np.float32),
        turn.imag.astype(np.float32),
        np.concatenate([bs_hi, bs_hi, bs_lo], 0),
        np.concatenate([bf_hi, bf_hi, bf_lo], 1),
    )


def split_terms(x):
    high = x.astype(jnp.bfloat16)
    low = (x - high.astype(jnp.float32)).astype(jnp.bfloat16)
    return high, low


def dot(left, right):
    return jnp.dot(left, right, preferred_element_type=jnp.float32)


def wide_dot(x, table):
    high, low = split_terms(x)
    return dot(jnp.concatenate([high, low, high], 1), table)


def prep_kernel(pairs, n_tables, values, filter_taps, cotangent, gate_acts, *rest):
    tables, rest = rest[:n_tables], rest[n_tables:]
    (narrow, wide, sems, table_sems), rest = rest[-4:], rest[:-4]
    outs, held = rest[: len(rest) - n_tables], rest[len(rest) - n_tables :]
    me = lax.axis_index("seq")
    channels = wide.shape[1] // 2
    n_steps = 2 * len(pairs)
    copies = []
    for at, j in enumerate(pairs):
        start = lax.bitwise_xor(lax.shift_right_logical(me, 1), j) * (2 * channels)
        both = pl.ds(pl.multiple_of(start, 2 * channels), 2 * channels)
        copies.append([pltpu.make_async_copy(filter_taps.at[both, :], wide.at[at], sems.at[at, 3])])
        for i, ref in enumerate((values, cotangent, gate_acts)):
            copies[-1].append(pltpu.make_async_copy(ref.at[both, :], narrow.at[at, i], sems.at[at, i]))
        for copy in copies[-1]:
            copy.start()
    brought = [
        pltpu.make_async_copy(tables[i].at[me] if i < 2 else tables[i], held[i], table_sems.at[i])
        for i in range(n_tables)
    ]
    for copy in brought:
        copy.start()
    for at in range(len(pairs)):
        for copy in copies[at]:
            copy.wait()
        for low in range(2):
            side = lax.bitwise_xor(lax.bitwise_and(me, 1), low) * channels
            mine = pl.ds(pl.multiple_of(side, channels), channels)
            blocks = [wide[at, mine, :], *(narrow[at, i, mine, :].astype(jnp.float32) for i in range(3))]
            for field, block in zip((TAPS, VALUE, COT, GATE), blocks):
                first = 0
                for out in outs[2 * at + low :: n_steps]:
                    size = out.shape[1]
                    out[field] = block[first : first + size].astype(jnp.bfloat16)
                    first += size
    for copy in brought:
        copy.wait()


def in_block(body):
    pl.when(lax.axis_index("seq") >= 0)(body)


def run_behind(tasks):
    tasks, live = list(tasks), []
    while tasks or live:
        live = [task for task in live if next(task, StopIteration) is None]
        if tasks:
            live.append(tasks.pop(0))
            next(live[-1])


def inverse(get, group, outer, turn, tables, put):
    (tr, ti), (bs3, bf3) = turn, tables
    high, low = split_terms(get())
    yield
    mid = dot(jnp.concatenate([high, low, high], 1), bs3[...])
    yield
    terms = []
    for pair in range(group // 2):
        cols = []
        for i in range(2):
            rows = slice((2 * pair + i) * outer, (2 * pair + i + 1) * outer)
            re, im = mid[rows, :LANES], mid[rows, LANES:]
            cols.append(jnp.concatenate([re * tr + im * ti, im * tr - re * ti], 0))
        terms.append(split_terms(jnp.concatenate(cols, 1)))
    yield
    ys = [dot(bf3[...], jnp.concatenate([high, low, high], 0)) for high, low in terms]
    yield
    for pair, y in enumerate(ys):
        for i in range(2):
            put(2 * pair + i, y[:, i * LANES : (i + 1) * LANES])
    yield


def taps_part(taps32, channels, source, part, own_outer):
    start = (source * own_outer + part) * (channels + PAD)
    start = pl.multiple_of(start, PAD) if channels % PAD == 0 else start
    return taps32[pl.ds(start, channels), :]


def mixer_kernel(n_seq, group, offset, places, last, *rest):
    blocks, rest = rest[:n_seq], rest[n_seq:]
    (f2, f3, s3, turn_re, turn_im, bs3, bf3), rest = rest[:7], rest[7:]
    if offset:
        rest = rest[1:]
    if last:
        grads, products, sig, taps, up, cot, grads32, grads16, sems = rest
    else:
        grads, taps_out, sig, taps, up, cot, grads32, grads16, sems, taps32 = rest
    me = lax.axis_index("seq")
    _, channels, seq_len = blocks[0].shape
    outer = sig.shape[0] // channels - PAD
    pitch, wide, narrow = outer + PAD, 2 * channels + PAD, channels + PAD
    own_outer = seq_len // LANES

    def stage(field, ref):
        for k in range(n_seq):
            for part in range(own_outer):
                cols = pl.ds(part * LANES, LANES)
                x = blocks[k][field, :, cols].astype(jnp.float32)
                rows = pl.ds(k * own_outer + part, channels, stride=pitch)
                if field == COT:
                    source = lax.bitwise_xor(me, k)
                    cot[pl.ds(source * own_outer + part, channels, stride=pitch), :] = x
                    x = x * blocks[k][GATE, :, cols].astype(jnp.float32)
                ref[rows, :] = x

    tr, ti = turn_re[...], turn_im[...]

    def forward(ref, field, base, out):
        exact = field != COT
        if base == 0:
            stage(field, ref)
        yield
        turned = []
        ys = []
        for pair in range(group // 2):
            xs = [ref[pl.ds((base + 2 * pair + i) * pitch, outer), :] for i in range(2)]
            x = jnp.concatenate(xs, 1)
            if exact:
                high = x.astype(jnp.bfloat16)
                ys.append(dot(f2[...], jnp.concatenate([high, high], 0)))
            else:
                high, low = split_terms(x)
                ys.append(dot(f3[...], jnp.concatenate([high, low, high], 0)))
        yield
        for y in ys:
            for i in range(2):
                re = y[:outer, i * LANES : (i + 1) * LANES]
                im = y[outer:, i * LANES : (i + 1) * LANES]
                turned.append(jnp.concatenate([re * tr - im * ti, re * ti + im * tr], 1))
        high, low = split_terms(jnp.concatenate(turned, 0))
        yield
        spec = dot(jnp.concatenate([high, low, high], 1), s3[...])
        out += [spec[:, :LANES], spec[:, LANES:]]
        yield

    def times(left, right, conj):
        (ar, ai), (br, bi) = left, right
        if conj:
            return jnp.concatenate([ar * br + ai * bi, ai * br - ar * bi], 1)
        return jnp.concatenate([ar * br - ai * bi, ar * bi + ai * br], 1)

    def backward(left, right, conj, base, put):
        yield
        yield from inverse(
            lambda: times(left, right, conj), group, outer, (tr, ti), (bs3, bf3), lambda ch, y: put(base + ch, y)
        )

    def keep_product(left, right, base):
        products[pl.ds(base * outer, group * outer), :] = times(left, right, True)
        yield

    copies = []

    def send(side):
        rows = slice(side * channels, (side + 1) * channels)
        for a in range(outer):
            grads16[side, places[a]] = grads32[a * wide + rows.start : a * wide + rows.stop, :].astype(jnp.bfloat16)
        to = grads.at[:, pl.ds(2 * offset + side * channels, channels), :]
        copies.append(pltpu.make_async_copy(grads16.at[side], to, sems.at[side]))
        copies[-1].start()

    def put_gate(ch, y):
        held = cot[pl.ds(ch * pitch, outer), :]
        grads32[pl.ds(channels + ch, outer, stride=wide), :] = y * held
        if ch == channels - 1:
            send(1)

    def put_value(ch, y):
        grads32[pl.ds(ch, outer, stride=wide), :] = y
        if ch == channels - 1:
            send(0)

    def put_taps(ch, y):
        taps32[pl.ds(ch, outer, stride=narrow), :] = y

    tasks = []
    for base in range(0, channels, group):
        k, v, u = [], [], []
        tasks += [
            forward(taps, TAPS, base, k),
            forward(sig, VALUE, base, v),
            forward(up, COT, base, u),
            backward(k, v, False, base, put_gate),
            backward(u, k, True, base, put_value),
            keep_product(u, v, base) if last else backward(u, v, True, base, put_taps),
        ]
    run_behind(tasks)

    if not last:
        for k in range(n_seq):
            source = lax.bitwise_xor(me, k)
            for part in range(own_outer):
                taps_out[k, :, pl.ds(part * LANES, LANES)] = taps_part(taps32, channels, source, part, own_outer)
    for copy in copies:
        copy.wait()


def lags_kernel(n_seq, group, channels, products, turn_re, turn_im, bs3, bf3, *rest):
    outs, taps32 = rest[-n_seq - 1 : -1], rest[-1]
    before = rest[: -n_seq - 1]
    me = lax.axis_index("seq")
    outer = products.shape[0] // channels
    own_outer = outs[0].shape[1] // LANES

    def put(ch, y):
        taps32[pl.ds(ch, outer, stride=channels + PAD), :] = y

    turn = turn_re[...], turn_im[...]

    def task(base):
        rows = pl.ds(base * outer, group * outer)
        return inverse(
            lambda: products[rows, :], group, outer, turn, (bs3, bf3), lambda ch, y: put(base + ch, y)
        )

    run_behind(task(base) for base in range(0, channels, group))
    for k in range(n_seq):
        source = lax.bitwise_xor(me, k)
        for part in range(own_outer):
            cols = pl.ds(part * LANES, LANES)
            parts = [x[k, :, cols] for x in before] + [taps_part(taps32, channels, source, part, own_outer)]
            outs[k][:, cols] = jnp.concatenate(parts, 0).astype(jnp.bfloat16)


def taps_kernel(n_seq, w_value, w_gate, *rest):
    taps_in, (out, w_held, sems) = rest[:n_seq], rest[n_seq:]
    me = lax.axis_index("seq")
    rows = w_value.shape[0]
    keep = w_held.shape[0] - rows
    copies = [
        pltpu.make_async_copy(w_value, w_held.at[:rows, :], sems.at[0]),
        pltpu.make_async_copy(w_gate.at[:keep, :], w_held.at[rows:, :], sems.at[1]),
    ]
    for copy in copies:
        copy.start()
    for k in range(n_seq):
        out[lax.bitwise_xor(me, k)] = taps_in[k][...].astype(jnp.float32)
    for copy in copies:
        copy.wait()


def project_kernel(n_seq, n_far, n_near, sizes, w_held, w_gate, spread, out, held, gate_held, total, sem):
    features = w_gate.shape[0]
    split = features - gate_held.shape[0]
    copy = pltpu.make_async_copy(w_gate.at[split:, :], gate_held, sem)
    copy.start()
    share = sum(sizes)
    firsts = [sum(sizes[:i]) for i in range(len(sizes))]

    def before():
        for source, (near, s, far) in enumerate(np.ndindex(n_near, n_seq, n_far)):
            block = spread[source].astype(jnp.float32)
            rows = pl.ds(((far * n_near + near) * n_seq + s) * share, share)
            for g in range(2):
                pieces = [block[2 * at + g * size : 2 * at + (g + 1) * size] for at, size in zip(firsts, sizes)]
                held[g, rows, :] = jnp.concatenate(pieces, 0).astype(held.dtype)
        values, gates = (held[g].astype(jnp.bfloat16) for g in range(2))
        total[...] = dot(w_held[:features, :], values)
        out[:, :split] = (total[:split, :] + dot(w_held[features:, :], gates)).T.astype(jnp.bfloat16)

    in_block(before)
    copy.wait()
    gates = held[1].astype(jnp.bfloat16)
    out[:, split:] = (total[split:, :] + dot(gate_held[...], gates)).T.astype(jnp.bfloat16)


def local(n_seq, n_far, n_near, values, gate_acts, cotangent, filter_taps, w_value, w_gate):
    rows, seq_len = values.shape
    n_chan = n_far * n_near
    total = seq_len * n_seq
    channels = rows // n_seq
    outer = total // LANES
    tokens = total // (n_seq * n_chan)
    me = lax.axis_index("seq")
    vmem = pl.BlockSpec(memory_space=pltpu.VMEM)
    hbm = pl.BlockSpec(memory_space=pltpu.HBM)

    def like(x):
        return pltpu.VMEM(x.shape, x.dtype)

    def stay(x):
        return pltpu.with_memory_space_constraint(x, pltpu.HBM)

    def route(k):
        return [(i, i ^ k) for i in range(n_seq)]

    sizes = (channels // 2, channels // 2) if channels % 32 == 0 else (channels,)
    chunks = len(sizes)
    tables = [jnp.asarray(t) for t in dft_tables(total, n_seq)]

    def prep(pairs, tables):
        steps = [2 * j + low for j in pairs for low in range(2)]
        outs = [pltpu.VMEM((4, size, seq_len), jnp.bfloat16) for size in sizes for _ in steps]
        outs += [pltpu.VMEM(t.shape[1:] if i < 2 else t.shape, t.dtype) for i, t in enumerate(tables)]
        ready = pl.pallas_call(
            functools.partial(prep_kernel, pairs, len(tables)),
            out_shape=outs,
            in_specs=[hbm] * (4 + len(tables)),
            out_specs=[vmem] * len(outs),
            scratch_shapes=[
                pltpu.VMEM((len(pairs), 3, 2 * channels, seq_len), jnp.bfloat16),
                pltpu.VMEM((len(pairs), 2 * channels, seq_len), jnp.float32),
                pltpu.SemaphoreType.DMA((len(pairs), 4)),
                pltpu.SemaphoreType.DMA((max(len(tables), 1),)),
            ],
            compiler_params=pltpu.CompilerParams(vmem_limit_bytes=8 * 2**20),
            cost_estimate=pl.CostEstimate(flops=0, bytes_accessed=4 * 2**20, transcendentals=0),
            name="prep",
        )(*(stay(x) for x in (values, filter_taps, cotangent, gate_acts, *tables)))
        for chunk in range(chunks):
            for at, k in enumerate(steps):
                sent[chunk, k] = ready[chunk * len(steps) + at]
        return ready[chunks * len(steps) :]

    sent, got = {}, {}
    if chunks > 1:
        prep(range(1, n_seq // 2), [])
        tables = prep((0,), tables)
    else:
        fields = (values, filter_taps.astype(jnp.bfloat16), cotangent, gate_acts)
        tables[:2] = [t[me] for t in tables[:2]]
        for k in range(n_seq):
            rows_k = [lax.dynamic_slice_in_dim(x, (me ^ k) * channels, channels, 0) for x in fields]
            sent[0, k] = jnp.stack(rows_k)
    for chunk in range(chunks):
        for k in reversed(range(n_seq)):
            block = sent[chunk, k]
            got[chunk, k] = lax.ppermute(block, "seq", route(k)) if k else block

    places = list(range(outer))
    if tokens == LANES:
        for s, far, near in np.ndindex(n_seq, n_far, n_near):
            places[(s * n_far + far) * n_near + near] = (near * n_seq + s) * n_far + far
    grads, before, offset = None, [], 0
    for chunk, size in enumerate(sizes):
        last = chunk == chunks - 1
        args = [*(got[chunk, k] for k in range(n_seq)), *tables]
        specs = [vmem] * len(args)
        aliases = {}
        if chunk:
            aliases = {len(args): 0}
            args.append(grads)
            specs.append(hbm)
        group = size if size <= 24 else 8
        long = pltpu.VMEM((size * (outer + PAD), LANES), jnp.float32)
        taps32 = pltpu.VMEM((outer * (size + PAD), LANES), jnp.float32)
        grads, more = pl.pallas_call(
            functools.partial(mixer_kernel, n_seq, group, offset, places, last),
            out_shape=[
                pltpu.HBM((outer, 2 * channels, LANES), jnp.bfloat16),
                pltpu.VMEM((size * outer, 2 * LANES) if last else (n_seq, size, seq_len), jnp.float32),
            ],
            in_specs=specs,
            out_specs=[hbm, vmem],
            input_output_aliases=aliases,
            scratch_shapes=[long] * 4
            + [
                pltpu.VMEM((outer * (2 * size + PAD), LANES), jnp.float32),
                pltpu.VMEM((2, outer, size, LANES), jnp.bfloat16),
                pltpu.SemaphoreType.DMA((2,)),
            ]
            + [taps32] * (not last),
            compiler_params=pltpu.CompilerParams(vmem_limit_bytes=24 * 2**20),
            cost_estimate=pl.CostEstimate(flops=5 * 10**9, bytes_accessed=2 * 2**20, transcendentals=0),
            name="mixer",
        )(*args)
        if not last:
            before.append(more)
        offset += size
    if tokens != LANES:
        grads = grads.reshape(outer, 2 * channels, LANES // tokens, tokens).transpose(0, 2, 1, 3)
        grads = grads.reshape(n_seq, n_far, n_near, 2 * channels, tokens).transpose(2, 0, 1, 3, 4)
        grads = grads.reshape(n_seq * n_chan, 2 * channels, tokens)
    spread = lax.all_to_all(grads, ("near", "seq", "far"), 0, 0, tiled=True)

    args = [more, *tables[3:], *before]
    taps_blocks = pl.pallas_call(
        functools.partial(lags_kernel, n_seq, group, size),
        out_shape=[jax.ShapeDtypeStruct((channels, seq_len), jnp.bfloat16)] * n_seq,
        in_specs=[vmem] * len(args),
        out_specs=[vmem] * n_seq,
        scratch_shapes=[taps32],
        compiler_params=pltpu.CompilerParams(vmem_limit_bytes=16 * 2**20),
        cost_estimate=pl.CostEstimate(flops=10**9, bytes_accessed=2**20, transcendentals=0),
        name="lags",
    )(*args)
    taps_got = [lax.ppermute(taps_blocks[k], "seq", route(k)) if k else taps_blocks[0] for k in range(n_seq)]
    taps_grad, w_held = pl.pallas_call(
        functools.partial(taps_kernel, n_seq),
        out_shape=[
            jax.ShapeDtypeStruct((n_seq, channels, seq_len), jnp.float32),
            pltpu.VMEM((w_value.shape[0] * (SLABS + KEPT) // SLABS, w_value.shape[1]), w_value.dtype),
        ],
        in_specs=[hbm] * 2 + [vmem] * n_seq,
        out_specs=[vmem] * 2,
        scratch_shapes=[pltpu.SemaphoreType.DMA((2,))],
        compiler_params=pltpu.CompilerParams(vmem_limit_bytes=8 * 2**20),
        name="taps",
    )(stay(w_value), stay(w_gate), *taps_got)

    held = jnp.bfloat16 if channels % 16 == 0 else jnp.float32
    args = [w_held, stay(w_gate), spread]
    input_grad = pl.pallas_call(
        functools.partial(project_kernel, n_seq, n_far, n_near, sizes),
        out_shape=jax.ShapeDtypeStruct((tokens, w_value.shape[0]), jnp.bfloat16),
        in_specs=[vmem, hbm, vmem],
        out_specs=vmem,
        scratch_shapes=[
            pltpu.VMEM((2, rows * n_chan, tokens), held),
            pltpu.VMEM((w_gate.shape[0] * (SLABS - KEPT) // SLABS, w_gate.shape[1]), w_gate.dtype),
            pltpu.VMEM((w_gate.shape[0], tokens), jnp.float32),
            pltpu.SemaphoreType.DMA,
        ],
        compiler_params=pltpu.CompilerParams(vmem_limit_bytes=16 * 2**20),
        name="project",
    )(*args)
    return input_grad, taps_grad.reshape(rows, seq_len)


def solution(mesh):
    n_seq, n_chan = mesh.shape["seq"], mesh.shape["chan"]
    n_far = math.gcd(n_chan, 4)
    parts = Mesh(mesh.devices.reshape(n_seq, n_far, n_chan // n_far), ("seq", "far", "near"))
    chan = ("far", "near")
    return jax.shard_map(
        functools.partial(local, n_seq, n_far, n_chan // n_far),
        mesh=parts,
        in_specs=(P(chan, "seq"), P(chan, "seq"), P(chan, "seq"), P(chan, "seq"), P(), P()),
        out_specs=(P(("seq", *chan), None), P(chan, "seq")),
        check_vma=False,
    )
```

```python
import functools
import math

import jax
import jax.numpy as jnp
import numpy as np
from jax import lax
from jax.experimental import pallas as pl
from jax.experimental.pallas import tpu as pltpu
from jax.sharding import Mesh
from jax.sharding import PartitionSpec as P

LANES = 128
VALUE, TAPS, COT, GATE = range(4)
SLABS = 8
KEPT = 3
PAD = 8


def halves(table):
    high = table.astype(jnp.bfloat16)
    low = (table - high.astype(np.float64)).astype(jnp.bfloat16)
    return high, low


def dft_tables(total, n_seq):
    outer = total // LANES
    k1 = np.arange(outer) + 0.25
    a = np.arange(outer)
    b = np.arange(LANES)
    first = np.exp(-2j * np.pi * np.outer(k1, a) / outer)
    first = np.concatenate([first.real, first.imag], 0)
    turn = np.exp(-2j * np.pi * np.outer(k1, b) / total)
    second = np.exp(-2j * np.pi * np.outer(b, b) / LANES)
    second = np.block([[second.real, second.imag], [-second.imag, second.real]])
    back_second = second.T / total / math.sqrt(total)
    back_first = np.exp(2j * np.pi * np.outer(a, k1) / outer)
    back_first = np.concatenate([back_first.real, -back_first.imag], 1)

    parts = first.reshape(2 * outer, n_seq, outer // n_seq)
    orders = np.arange(n_seq)[:, None] ^ np.arange(n_seq)
    first = np.stack([parts[:, order].reshape(2 * outer, outer) for order in orders])
    f_hi, f_lo = halves(first)
    s_hi, s_lo = halves(second)
    bs_hi, bs_lo = halves(back_second)
    bf_hi, bf_lo = halves(back_first)
    return (
        np.concatenate([f_hi, f_lo], 2),
        np.concatenate([f_hi, f_hi, f_lo], 2),
        np.concatenate([s_hi, s_hi, s_lo], 0),
        turn.real.astype(np.float32),
        turn.imag.astype(np.float32),
        np.concatenate([bs_hi, bs_hi, bs_lo], 0),
        np.concatenate([bf_hi, bf_hi, bf_lo], 1),
    )


def split_terms(x):
    high = x.astype(jnp.bfloat16)
    low = (x - high.astype(jnp.float32)).astype(jnp.bfloat16)
    return high, low


def dot(left, right):
    return jnp.dot(left, right, preferred_element_type=jnp.float32)


def wide_dot(x, table):
    high, low = split_terms(x)
    return dot(jnp.concatenate([high, low, high], 1), table)


def prep_kernel(jobs, n_tables, values, filter_taps, cotangent, gate_acts, *rest):
    tables, rest = rest[:n_tables], rest[n_tables:]
    (narrow, wide, sems, table_sems), rest = rest[-4:], rest[:-4]
    outs, held = rest[: 2 * len(jobs)], rest[2 * len(jobs) :]
    me = lax.axis_index("seq")
    copies = []
    for at, (j, chunk) in enumerate(jobs):
        both = pl.ds(lax.bitwise_xor(lax.shift_right_logical(me, 1), j) * 2, 2)
        copies.append([pltpu.make_async_copy(filter_taps.at[both, chunk], wide.at[at], sems.at[at, 3])])
        for i, ref in enumerate((values, cotangent, gate_acts)):
            copies[-1].append(pltpu.make_async_copy(ref.at[both, chunk], narrow.at[at, i], sems.at[at, i]))
        for copy in copies[-1]:
            copy.start()
    brought = [
        pltpu.make_async_copy(tables[i].at[me] if i < 2 else tables[i], held[i], table_sems.at[i])
        for i in range(n_tables)
    ]
    for copy in brought:
        copy.start()
    for at in range(len(jobs)):
        for copy in copies[at]:
            copy.wait()
        for low in range(2):
            side = lax.bitwise_xor(lax.bitwise_and(me, 1), low)
            out = outs[2 * at + low]
            out[TAPS] = wide[at, side].astype(jnp.bfloat16)
            for i, field in enumerate((VALUE, COT, GATE)):
                out[field] = narrow[at, i, side]
    for copy in brought:
        copy.wait()


def in_block(body):
    pl.when(lax.axis_index("seq") >= 0)(body)


def run_behind(tasks):
    tasks, live = list(tasks), []
    while tasks or live:
        live = [task for task in live if next(task, StopIteration) is None]
        if tasks:
            live.append(tasks.pop(0))
            next(live[-1])


def inverse(get, group, outer, turn, tables, put):
    (tr, ti), (bs3, bf3) = turn, tables
    high, low = split_terms(get())
    yield
    mid = dot(jnp.concatenate([high, low, high], 1), bs3[...])
    yield
    terms = []
    for pair in range(group // 2):
        cols = []
        for i in range(2):
            rows = slice((2 * pair + i) * outer, (2 * pair + i + 1) * outer)
            re, im = mid[rows, :LANES], mid[rows, LANES:]
            cols.append(jnp.concatenate([re * tr + im * ti, im * tr - re * ti], 0))
        terms.append(split_terms(jnp.concatenate(cols, 1)))
    yield
    ys = [dot(bf3[...], jnp.concatenate([high, low, high], 0)) for high, low in terms]
    yield
    for pair, y in enumerate(ys):
        for i in range(2):
            put(2 * pair + i, y[:, i * LANES : (i + 1) * LANES])
    yield


def taps_part(taps32, channels, source, part, own_outer):
    start = (source * own_outer + part) * (channels + PAD)
    start = pl.multiple_of(start, PAD) if channels % PAD == 0 else start
    return taps32[pl.ds(start, channels), :]


def mixer_kernel(n_seq, group, offset, places, last, *rest):
    blocks, rest = rest[:n_seq], rest[n_seq:]
    (f2, f3, s3, turn_re, turn_im, bs3, bf3), rest = rest[:7], rest[7:]
    if offset:
        rest = rest[1:]
    if last:
        grads, products, sig, taps, up, cot, grads32, grads16, sems = rest
    else:
        grads, taps_out, sig, taps, up, cot, grads32, grads16, sems, taps32 = rest
    me = lax.axis_index("seq")
    _, channels, seq_len = blocks[0].shape
    outer = sig.shape[0] // channels - PAD
    pitch, wide, narrow = outer + PAD, 2 * channels + PAD, channels + PAD
    own_outer = seq_len // LANES

    def stage(field, ref):
        for k in range(n_seq):
            for part in range(own_outer):
                cols = pl.ds(part * LANES, LANES)
                x = blocks[k][field, :, cols].astype(jnp.float32)
                rows = pl.ds(k * own_outer + part, channels, stride=pitch)
                if field == COT:
                    source = lax.bitwise_xor(me, k)
                    cot[pl.ds(source * own_outer + part, channels, stride=pitch), :] = x
                    x = x * blocks[k][GATE, :, cols].astype(jnp.float32)
                ref[rows, :] = x

    tr, ti = turn_re[...], turn_im[...]

    def forward(ref, field, base, out):
        exact = field != COT
        if base == 0:
            stage(field, ref)
        yield
        turned = []
        ys = []
        for pair in range(group // 2):
            xs = [ref[pl.ds((base + 2 * pair + i) * pitch, outer), :] for i in range(2)]
            x = jnp.concatenate(xs, 1)
            if exact:
                high = x.astype(jnp.bfloat16)
                ys.append(dot(f2[...], jnp.concatenate([high, high], 0)))
            else:
                high, low = split_terms(x)
                ys.append(dot(f3[...], jnp.concatenate([high, low, high], 0)))
        yield
        for y in ys:
            for i in range(2):
                re = y[:outer, i * LANES : (i + 1) * LANES]
                im = y[outer:, i * LANES : (i + 1) * LANES]
                turned.append(jnp.concatenate([re * tr - im * ti, re * ti + im * tr], 1))
        high, low = split_terms(jnp.concatenate(turned, 0))
        yield
        spec = dot(jnp.concatenate([high, low, high], 1), s3[...])
        out += [spec[:, :LANES], spec[:, LANES:]]
        yield

    def times(left, right, conj):
        (ar, ai), (br, bi) = left, right
        if conj:
            return jnp.concatenate([ar * br + ai * bi, ai * br - ar * bi], 1)
        return jnp.concatenate([ar * br - ai * bi, ar * bi + ai * br], 1)

    def backward(left, right, conj, base, put):
        yield
        yield from inverse(
            lambda: times(left, right, conj), group, outer, (tr, ti), (bs3, bf3), lambda ch, y: put(base + ch, y)
        )

    def keep_product(left, right, base):
        products[pl.ds(base * outer, group * outer), :] = times(left, right, True)
        yield

    copies = []

    def send(side):
        rows = slice(side * channels, (side + 1) * channels)
        for a in range(outer):
            grads16[side, places[a]] = grads32[a * wide + rows.start : a * wide + rows.stop, :].astype(jnp.bfloat16)
        to = grads.at[:, pl.ds(2 * offset + side * channels, channels), :]
        copies.append(pltpu.make_async_copy(grads16.at[side], to, sems.at[side]))
        copies[-1].start()

    def put_gate(ch, y):
        held = cot[pl.ds(ch * pitch, outer), :]
        grads32[pl.ds(channels + ch, outer, stride=wide), :] = y * held
        if ch == channels - 1:
            send(1)

    def put_value(ch, y):
        grads32[pl.ds(ch, outer, stride=wide), :] = y
        if ch == channels - 1:
            send(0)

    def put_taps(ch, y):
        taps32[pl.ds(ch, outer, stride=narrow), :] = y

    tasks = []
    for base in range(0, channels, group):
        k, v, u = [], [], []
        tasks += [
            forward(taps, TAPS, base, k),
            forward(sig, VALUE, base, v),
            forward(up, COT, base, u),
            backward(k, v, False, base, put_gate),
            backward(u, k, True, base, put_value),
            keep_product(u, v, base) if last else backward(u, v, True, base, put_taps),
        ]
    run_behind(tasks)

    if not last:
        for k in range(n_seq):
            source = lax.bitwise_xor(me, k)
            for part in range(own_outer):
                taps_out[k, :, pl.ds(part * LANES, LANES)] = taps_part(taps32, channels, source, part, own_outer)
    for copy in copies:
        copy.wait()


def lags_kernel(n_seq, group, channels, products, turn_re, turn_im, bs3, bf3, *rest):
    outs, taps32 = rest[-n_seq - 1 : -1], rest[-1]
    before = rest[: -n_seq - 1]
    me = lax.axis_index("seq")
    outer = products.shape[0] // channels
    own_outer = outs[0].shape[1] // LANES

    def put(ch, y):
        taps32[pl.ds(ch, outer, stride=channels + PAD), :] = y

    turn = turn_re[...], turn_im[...]

    def task(base):
        rows = pl.ds(base * outer, group * outer)
        return inverse(
            lambda: products[rows, :], group, outer, turn, (bs3, bf3), lambda ch, y: put(base + ch, y)
        )

    run_behind(task(base) for base in range(0, channels, group))
    for k in range(n_seq):
        source = lax.bitwise_xor(me, k)
        for part in range(own_outer):
            cols = pl.ds(part * LANES, LANES)
            parts = [x[k, :, cols] for x in before] + [taps_part(taps32, channels, source, part, own_outer)]
            outs[k][:, cols] = jnp.concatenate(parts, 0).astype(jnp.bfloat16)


def taps_kernel(n_seq, w_value, w_gate, *rest):
    taps_in, (out, w_held, sems) = rest[:n_seq], rest[n_seq:]
    me = lax.axis_index("seq")
    rows = w_value.shape[0]
    keep = w_held.shape[0] - rows
    copies = [
        pltpu.make_async_copy(w_value, w_held.at[:rows, :], sems.at[0]),
        pltpu.make_async_copy(w_gate.at[:keep, :], w_held.at[rows:, :], sems.at[1]),
    ]
    for copy in copies:
        copy.start()
    for k in range(n_seq):
        out[lax.bitwise_xor(me, k)] = taps_in[k][...].astype(jnp.float32)
    for copy in copies:
        copy.wait()


def project_kernel(n_seq, n_far, n_near, sizes, w_held, w_gate, spread, out, held, gate_held, total, sem):
    features = w_gate.shape[0]
    split = features - gate_held.shape[0]
    copy = pltpu.make_async_copy(w_gate.at[split:, :], gate_held, sem)
    copy.start()
    share = sum(sizes)
    firsts = [sum(sizes[:i]) for i in range(len(sizes))]

    def before():
        for source, (near, s, far) in enumerate(np.ndindex(n_near, n_seq, n_far)):
            block = spread[source].astype(jnp.float32)
            rows = pl.ds(((far * n_near + near) * n_seq + s) * share, share)
            for g in range(2):
                pieces = [block[2 * at + g * size : 2 * at + (g + 1) * size] for at, size in zip(firsts, sizes)]
                held[g, rows, :] = jnp.concatenate(pieces, 0).astype(held.dtype)
        values, gates = (held[g].astype(jnp.bfloat16) for g in range(2))
        total[...] = dot(w_held[:features, :], values)
        out[:, :split] = (total[:split, :] + dot(w_held[features:, :], gates)).T.astype(jnp.bfloat16)

    in_block(before)
    copy.wait()
    gates = held[1].astype(jnp.bfloat16)
    out[:, split:] = (total[split:, :] + dot(gate_held[...], gates)).T.astype(jnp.bfloat16)


def local(n_seq, n_far, n_near, values, gate_acts, cotangent, filter_taps, w_value, w_gate):
    rows, seq_len = values.shape
    n_chan = n_far * n_near
    total = seq_len * n_seq
    channels = rows // n_seq
    outer = total // LANES
    tokens = total // (n_seq * n_chan)
    me = lax.axis_index("seq")
    vmem = pl.BlockSpec(memory_space=pltpu.VMEM)
    hbm = pl.BlockSpec(memory_space=pltpu.HBM)

    def like(x):
        return pltpu.VMEM(x.shape, x.dtype)

    def stay(x):
        return pltpu.with_memory_space_constraint(x, pltpu.HBM)

    def route(k):
        return [(i, i ^ k) for i in range(n_seq)]

    sizes = (channels // 2, channels // 2) if channels % 32 == 0 else (channels,)
    chunks = len(sizes)
    tables = [jnp.asarray(t) for t in dft_tables(total, n_seq)]

    def prep(jobs, tables):
        size = channels // chunks
        outs = [pltpu.VMEM((4, size, seq_len), jnp.bfloat16)] * (2 * len(jobs))
        outs += [pltpu.VMEM(t.shape[1:] if i < 2 else t.shape, t.dtype) for i, t in enumerate(tables)]
        fields = [
            x.reshape(n_seq, chunks, size, seq_len) for x in (values, filter_taps, cotangent, gate_acts)
        ]
        ready = pl.pallas_call(
            functools.partial(prep_kernel, jobs, len(tables)),
            out_shape=outs,
            in_specs=[hbm] * (4 + len(tables)),
            out_specs=[vmem] * len(outs),
            scratch_shapes=[
                pltpu.VMEM((len(jobs), 3, 2, size, seq_len), jnp.bfloat16),
                pltpu.VMEM((len(jobs), 2, size, seq_len), jnp.float32),
                pltpu.SemaphoreType.DMA((len(jobs), 4)),
                pltpu.SemaphoreType.DMA((max(len(tables), 1),)),
            ],
            compiler_params=pltpu.CompilerParams(vmem_limit_bytes=8 * 2**20),
            cost_estimate=pl.CostEstimate(flops=0, bytes_accessed=4 * 2**20, transcendentals=0),
            name="prep",
        )(*(stay(x) for x in (*fields, *tables)))
        for at, (j, chunk) in enumerate(jobs):
            for low in range(2):
                sent[chunk, 2 * j + low] = ready[2 * at + low]
        return ready[2 * len(jobs) :]

    sent, got = {}, {}
    if chunks > 1 and n_seq > 2:
        jobs = [(j, chunk) for chunk in range(chunks) for j in reversed(range(n_seq // 2))]
        prep(jobs[: n_seq // 2 - 1], [])
        tables = prep(jobs[n_seq // 2 - 1 :], tables)
    else:
        fields = (values, filter_taps.astype(jnp.bfloat16), cotangent, gate_acts)
        tables[:2] = [t[me] for t in tables[:2]]
        for k in range(n_seq):
            rows_k = [lax.dynamic_slice_in_dim(x, (me ^ k) * channels, channels, 0) for x in fields]
            sent[0, k] = jnp.stack(rows_k)
    for chunk in range(chunks):
        for k in reversed(range(n_seq)):
            block = sent[chunk, k]
            got[chunk, k] = lax.ppermute(block, "seq", route(k)) if k else block

    places = list(range(outer))
    if tokens == LANES:
        for s, far, near in np.ndindex(n_seq, n_far, n_near):
            places[(s * n_far + far) * n_near + near] = (near * n_seq + s) * n_far + far
    grads, before, offset = None, [], 0
    for chunk, size in enumerate(sizes):
        last = chunk == chunks - 1
        args = [*(got[chunk, k] for k in range(n_seq)), *tables]
        specs = [vmem] * len(args)
        aliases = {}
        if chunk:
            aliases = {len(args): 0}
            args.append(grads)
            specs.append(hbm)
        group = size if size <= 24 else 8
        long = pltpu.VMEM((size * (outer + PAD), LANES), jnp.float32)
        taps32 = pltpu.VMEM((outer * (size + PAD), LANES), jnp.float32)
        grads, more = pl.pallas_call(
            functools.partial(mixer_kernel, n_seq, group, offset, places, last),
            out_shape=[
                pltpu.HBM((outer, 2 * channels, LANES), jnp.bfloat16),
                pltpu.VMEM((size * outer, 2 * LANES) if last else (n_seq, size, seq_len), jnp.float32),
            ],
            in_specs=specs,
            out_specs=[hbm, vmem],
            input_output_aliases=aliases,
            scratch_shapes=[long] * 4
            + [
                pltpu.VMEM((outer * (2 * size + PAD), LANES), jnp.float32),
                pltpu.VMEM((2, outer, size, LANES), jnp.bfloat16),
                pltpu.SemaphoreType.DMA((2,)),
            ]
            + [taps32] * (not last),
            compiler_params=pltpu.CompilerParams(vmem_limit_bytes=24 * 2**20),
            cost_estimate=pl.CostEstimate(flops=5 * 10**9, bytes_accessed=2 * 2**20, transcendentals=0),
            name="mixer",
        )(*args)
        if not last:
            before.append(more)
        offset += size
    if tokens != LANES:
        grads = grads.reshape(outer, 2 * channels, LANES // tokens, tokens).transpose(0, 2, 1, 3)
        grads = grads.reshape(n_seq, n_far, n_near, 2 * channels, tokens).transpose(2, 0, 1, 3, 4)
        grads = grads.reshape(n_seq * n_chan, 2 * channels, tokens)
    spread = lax.all_to_all(grads, ("near", "seq", "far"), 0, 0, tiled=True)

    args = [more, *tables[3:], *before]
    taps_blocks = pl.pallas_call(
        functools.partial(lags_kernel, n_seq, group, size),
        out_shape=[jax.ShapeDtypeStruct((channels, seq_len), jnp.bfloat16)] * n_seq,
        in_specs=[vmem] * len(args),
        out_specs=[vmem] * n_seq,
        scratch_shapes=[taps32],
        compiler_params=pltpu.CompilerParams(vmem_limit_bytes=16 * 2**20),
        cost_estimate=pl.CostEstimate(flops=10**9, bytes_accessed=2**20, transcendentals=0),
        name="lags",
    )(*args)
    taps_got = [lax.ppermute(taps_blocks[k], "seq", route(k)) if k else taps_blocks[0] for k in range(n_seq)]
    taps_grad, w_held = pl.pallas_call(
        functools.partial(taps_kernel, n_seq),
        out_shape=[
            jax.ShapeDtypeStruct((n_seq, channels, seq_len), jnp.float32),
            pltpu.VMEM((w_value.shape[0] * (SLABS + KEPT) // SLABS, w_value.shape[1]), w_value.dtype),
        ],
        in_specs=[hbm] * 2 + [vmem] * n_seq,
        out_specs=[vmem] * 2,
        scratch_shapes=[pltpu.SemaphoreType.DMA((2,))],
        compiler_params=pltpu.CompilerParams(vmem_limit_bytes=8 * 2**20),
        name="taps",
    )(stay(w_value), stay(w_gate), *taps_got)

    held = jnp.bfloat16 if channels % 16 == 0 else jnp.float32
    args = [w_held, stay(w_gate), spread]
    input_grad = pl.pallas_call(
        functools.partial(project_kernel, n_seq, n_far, n_near, sizes),
        out_shape=jax.ShapeDtypeStruct((tokens, w_value.shape[0]), jnp.bfloat16),
        in_specs=[vmem, hbm, vmem],
        out_specs=vmem,
        scratch_shapes=[
            pltpu.VMEM((2, rows * n_chan, tokens), held),
            pltpu.VMEM((w_gate.shape[0] * (SLABS - KEPT) // SLABS, w_gate.shape[1]), w_gate.dtype),
            pltpu.VMEM((w_gate.shape[0], tokens), jnp.float32),
            pltpu.SemaphoreType.DMA,
        ],
        compiler_params=pltpu.CompilerParams(vmem_limit_bytes=16 * 2**20),
        name="project",
    )(*args)
    return input_grad, taps_grad.reshape(rows, seq_len)


def solution(mesh):
    n_seq, n_chan = mesh.shape["seq"], mesh.shape["chan"]
    n_far = math.gcd(n_chan, 4)
    parts = Mesh(mesh.devices.reshape(n_seq, n_far, n_chan // n_far), ("seq", "far", "near"))
    chan = ("far", "near")
    return jax.shard_map(
        functools.partial(local, n_seq, n_far, n_chan // n_far),
        mesh=parts,
        in_specs=(P(chan, "seq"), P(chan, "seq"), P(chan, "seq"), P(chan, "seq"), P(), P()),
        out_specs=(P(("seq", *chan), None), P(chan, "seq")),
        check_vma=False,
    )
```

```python
import functools
import math

import jax
import jax.numpy as jnp
import numpy as np
from jax import lax
from jax.experimental import pallas as pl
from jax.experimental.pallas import tpu as pltpu
from jax.sharding import Mesh
from jax.sharding import PartitionSpec as P

LANES = 128
VALUE, TAPS, COT, GATE = range(4)
SLABS = 8
KEPT = 3
PAD = 8


def halves(table):
    high = table.astype(jnp.bfloat16)
    low = (table - high.astype(np.float64)).astype(jnp.bfloat16)
    return high, low


def dft_tables(total, n_seq):
    outer = total // LANES
    k1 = np.arange(outer) + 0.25
    a = np.arange(outer)
    b = np.arange(LANES)
    first = np.exp(-2j * np.pi * np.outer(k1, a) / outer)
    first = np.concatenate([first.real, first.imag], 0)
    turn = np.exp(-2j * np.pi * np.outer(k1, b) / total)
    second = np.exp(-2j * np.pi * np.outer(b, b) / LANES)
    second = np.block([[second.real, second.imag], [-second.imag, second.real]])
    back_second = second.T / total / math.sqrt(total)
    back_first = np.exp(2j * np.pi * np.outer(a, k1) / outer)
    back_first = np.concatenate([back_first.real, -back_first.imag], 1)

    parts = first.reshape(2 * outer, n_seq, outer // n_seq)
    orders = np.arange(n_seq)[:, None] ^ np.arange(n_seq)
    first = np.stack([parts[:, order].reshape(2 * outer, outer) for order in orders])
    f_hi, f_lo = halves(first)
    s_hi, s_lo = halves(second)
    bs_hi, bs_lo = halves(back_second)
    bf_hi, bf_lo = halves(back_first)
    return (
        np.concatenate([f_hi, f_lo], 2),
        np.concatenate([f_hi, f_hi, f_lo], 2),
        np.concatenate([s_hi, s_hi, s_lo], 0),
        turn.real.astype(np.float32),
        turn.imag.astype(np.float32),
        np.concatenate([bs_hi, bs_hi, bs_lo], 0),
        np.concatenate([bf_hi, bf_hi, bf_lo], 1),
    )


def split_terms(x):
    high = x.astype(jnp.bfloat16)
    low = (x - high.astype(jnp.float32)).astype(jnp.bfloat16)
    return high, low


def dot(left, right):
    return jnp.dot(left, right, preferred_element_type=jnp.float32)


def wide_dot(x, table):
    high, low = split_terms(x)
    return dot(jnp.concatenate([high, low, high], 1), table)


def prep_kernel(jobs, n_tables, values, filter_taps, cotangent, gate_acts, *rest):
    tables, rest = rest[:n_tables], rest[n_tables:]
    (narrow, wide, sems, table_sems), rest = rest[-4:], rest[:-4]
    outs, held = rest[: 2 * len(jobs)], rest[2 * len(jobs) :]
    me = lax.axis_index("seq")
    copies = []
    for at, (j, chunk) in enumerate(jobs):
        both = pl.ds(lax.bitwise_xor(lax.shift_right_logical(me, 1), j) * 2, 2)
        copies.append([pltpu.make_async_copy(filter_taps.at[both, chunk], wide.at[at], sems.at[at, 3])])
        for i, ref in enumerate((values, cotangent, gate_acts)):
            copies[-1].append(pltpu.make_async_copy(ref.at[both, chunk], narrow.at[at, i], sems.at[at, i]))
        for copy in copies[-1]:
            copy.start()
    brought = [
        pltpu.make_async_copy(tables[i].at[me] if i < 2 else tables[i], held[i], table_sems.at[i])
        for i in range(n_tables)
    ]
    for copy in brought:
        copy.start()
    for at in range(len(jobs)):
        for copy in copies[at]:
            copy.wait()
        for low in range(2):
            side = lax.bitwise_xor(lax.bitwise_and(me, 1), low)
            out = outs[2 * at + low]
            out[TAPS] = wide[at, side].astype(jnp.bfloat16)
            for i, field in enumerate((VALUE, COT, GATE)):
                out[field] = narrow[at, i, side]
    for copy in brought:
        copy.wait()


def in_block(body):
    pl.when(lax.axis_index("seq") >= 0)(body)


def run_behind(tasks):
    tasks, live = list(tasks), []
    while tasks or live:
        live = [task for task in live if next(task, StopIteration) is None]
        if tasks:
            live.append(tasks.pop(0))
            next(live[-1])


def inverse(get, group, outer, turn, tables, put):
    (tr, ti), (bs3, bf3) = turn, tables
    high, low = split_terms(get())
    yield
    mid = dot(jnp.concatenate([high, low, high], 1), bs3[...])
    yield
    terms = []
    for pair in range(group // 2):
        cols = []
        for i in range(2):
            rows = slice((2 * pair + i) * outer, (2 * pair + i + 1) * outer)
            re, im = mid[rows, :LANES], mid[rows, LANES:]
            cols.append(jnp.concatenate([re * tr + im * ti, im * tr - re * ti], 0))
        terms.append(split_terms(jnp.concatenate(cols, 1)))
    yield
    ys = [dot(bf3[...], jnp.concatenate([high, low, high], 0)) for high, low in terms]
    yield
    for pair, y in enumerate(ys):
        for i in range(2):
            put(2 * pair + i, y[:, i * LANES : (i + 1) * LANES])
    yield


def taps_part(taps32, channels, source, part, own_outer):
    start = (source * own_outer + part) * (channels + PAD)
    start = pl.multiple_of(start, PAD) if channels % PAD == 0 else start
    return taps32[pl.ds(start, channels), :]


def mixer_kernel(n_seq, group, offset, places, last, *rest):
    blocks, rest = rest[:n_seq], rest[n_seq:]
    (f2, f3, s3, turn_re, turn_im, bs3, bf3), rest = rest[:7], rest[7:]
    if offset:
        rest = rest[1:]
    if last:
        grads, products, sig, taps, up, cot, grads32, grads16, sems = rest
    else:
        grads, taps_out, sig, taps, up, cot, grads32, grads16, sems, taps32 = rest
    me = lax.axis_index("seq")
    _, channels, seq_len = blocks[0].shape
    outer = grads.shape[0]
    pitch, wide, narrow = outer + PAD, 2 * channels + PAD, channels + PAD
    own_outer = seq_len // LANES

    def stage(field, ref):
        for k in range(n_seq):
            for part in range(own_outer):
                cols = pl.ds(part * LANES, LANES)
                x = blocks[k][field, :, cols].astype(jnp.float32)
                rows = pl.ds(k * own_outer + part, channels, stride=pitch)
                if field == COT:
                    source = lax.bitwise_xor(me, k)
                    cot[pl.ds(source * own_outer + part, channels, stride=pitch), :] = x
                    x = x * blocks[k][GATE, :, cols].astype(jnp.float32)
                ref[rows, :] = x

    tr, ti = turn_re[...], turn_im[...]

    def forward(ref, field, base, out):
        exact = field != COT
        if base == 0:
            stage(field, ref)
        yield
        turned = []
        ys = []
        for pair in range(group // 2):
            xs = [ref[pl.ds((base + 2 * pair + i) * pitch, outer), :] for i in range(2)]
            x = jnp.concatenate(xs, 1)
            if exact:
                high = x.astype(jnp.bfloat16)
                ys.append(dot(f2[...], jnp.concatenate([high, high], 0)))
            else:
                high, low = split_terms(x)
                ys.append(dot(f3[...], jnp.concatenate([high, low, high], 0)))
        yield
        for y in ys:
            for i in range(2):
                re = y[:outer, i * LANES : (i + 1) * LANES]
                im = y[outer:, i * LANES : (i + 1) * LANES]
                turned.append(jnp.concatenate([re * tr - im * ti, re * ti + im * tr], 1))
        high, low = split_terms(jnp.concatenate(turned, 0))
        yield
        spec = dot(jnp.concatenate([high, low, high], 1), s3[...])
        out += [spec[:, :LANES], spec[:, LANES:]]
        yield

    def times(left, right, conj):
        (ar, ai), (br, bi) = left, right
        if conj:
            return jnp.concatenate([ar * br + ai * bi, ai * br - ar * bi], 1)
        return jnp.concatenate([ar * br - ai * bi, ar * bi + ai * br], 1)

    def backward(left, right, conj, base, put):
        yield
        yield from inverse(
            lambda: times(left, right, conj), group, outer, (tr, ti), (bs3, bf3), lambda ch, y: put(base + ch, y)
        )

    def keep_product(left, right, base):
        products[pl.ds(base * outer, group * outer), :] = times(left, right, True)
        yield

    copies = []

    def send(side):
        rows = slice(side * channels, (side + 1) * channels)
        for a in range(outer):
            grads16[side, places[a]] = grads32[a * wide + rows.start : a * wide + rows.stop, :].astype(jnp.bfloat16)
        to = grads.at[:, pl.ds(2 * offset + side * channels, channels), :]
        copies.append(pltpu.make_async_copy(grads16.at[side], to, sems.at[side]))
        copies[-1].start()

    def put_gate(ch, y):
        held = cot[pl.ds(ch * pitch, outer), :]
        grads32[pl.ds(channels + ch, outer, stride=wide), :] = y * held
        if ch == channels - 1:
            send(1)

    def put_value(ch, y):
        grads32[pl.ds(ch, outer, stride=wide), :] = y
        if ch == channels - 1:
            send(0)

    def put_taps(ch, y):
        taps32[pl.ds(ch, outer, stride=narrow), :] = y

    tasks = []
    for base in range(0, channels, group):
        k, v, u = [], [], []
        tasks += [
            forward(taps, TAPS, base, k),
            forward(sig, VALUE, base, v),
            forward(up, COT, base, u),
            backward(k, v, False, base, put_gate),
            backward(u, k, True, base, put_value),
            keep_product(u, v, base) if last else backward(u, v, True, base, put_taps),
        ]
    run_behind(tasks)

    if not last:
        for k in range(n_seq):
            source = lax.bitwise_xor(me, k)
            for part in range(own_outer):
                taps_out[k, :, pl.ds(part * LANES, LANES)] = taps_part(taps32, channels, source, part, own_outer)
    for copy in copies:
        copy.wait()


def lags_kernel(n_seq, group, channels, products, turn_re, turn_im, bs3, bf3, *rest):
    outs, taps32 = rest[-n_seq - 1 : -1], rest[-1]
    before = rest[: -n_seq - 1]
    me = lax.axis_index("seq")
    outer = products.shape[0] // channels
    own_outer = outs[0].shape[1] // LANES

    def put(ch, y):
        taps32[pl.ds(ch, outer, stride=channels + PAD), :] = y

    turn = turn_re[...], turn_im[...]

    def task(base):
        rows = pl.ds(base * outer, group * outer)
        return inverse(
            lambda: products[rows, :], group, outer, turn, (bs3, bf3), lambda ch, y: put(base + ch, y)
        )

    run_behind(task(base) for base in range(0, channels, group))
    for k in range(n_seq):
        source = lax.bitwise_xor(me, k)
        for part in range(own_outer):
            cols = pl.ds(part * LANES, LANES)
            parts = [x[k, :, cols] for x in before] + [taps_part(taps32, channels, source, part, own_outer)]
            outs[k][:, cols] = jnp.concatenate(parts, 0).astype(jnp.bfloat16)


def taps_kernel(n_seq, w_value, w_gate, *rest):
    taps_in, (out, w_held, sems) = rest[:n_seq], rest[n_seq:]
    me = lax.axis_index("seq")
    rows = w_value.shape[0]
    keep = w_held.shape[0] - rows
    copies = [
        pltpu.make_async_copy(w_value, w_held.at[:rows, :], sems.at[0]),
        pltpu.make_async_copy(w_gate.at[:keep, :], w_held.at[rows:, :], sems.at[1]),
    ]
    for copy in copies:
        copy.start()
    for k in range(n_seq):
        out[lax.bitwise_xor(me, k)] = taps_in[k][...].astype(jnp.float32)
    for copy in copies:
        copy.wait()


def project_kernel(n_seq, n_far, n_near, sizes, w_held, w_gate, spread, out, held, gate_held, total, sem):
    features = w_gate.shape[0]
    split = features - gate_held.shape[0]
    copy = pltpu.make_async_copy(w_gate.at[split:, :], gate_held, sem)
    copy.start()
    share = sum(sizes)
    firsts = [sum(sizes[:i]) for i in range(len(sizes))]

    def before():
        for source, (near, s, far) in enumerate(np.ndindex(n_near, n_seq, n_far)):
            block = spread[source].astype(jnp.float32)
            rows = pl.ds(((far * n_near + near) * n_seq + s) * share, share)
            for g in range(2):
                pieces = [block[2 * at + g * size : 2 * at + (g + 1) * size] for at, size in zip(firsts, sizes)]
                held[g, rows, :] = jnp.concatenate(pieces, 0).astype(held.dtype)
        values, gates = (held[g].astype(jnp.bfloat16) for g in range(2))
        total[...] = dot(w_held[:features, :], values)
        out[:, :split] = (total[:split, :] + dot(w_held[features:, :], gates)).T.astype(jnp.bfloat16)

    in_block(before)
    copy.wait()
    gates = held[1].astype(jnp.bfloat16)
    out[:, split:] = (total[split:, :] + dot(gate_held[...], gates)).T.astype(jnp.bfloat16)


def local(n_seq, n_far, n_near, values, gate_acts, cotangent, filter_taps, w_value, w_gate):
    rows, seq_len = values.shape
    n_chan = n_far * n_near
    total = seq_len * n_seq
    channels = rows // n_seq
    outer = total // LANES
    tokens = total // (n_seq * n_chan)
    me = lax.axis_index("seq")
    vmem = pl.BlockSpec(memory_space=pltpu.VMEM)
    hbm = pl.BlockSpec(memory_space=pltpu.HBM)

    def like(x):
        return pltpu.VMEM(x.shape, x.dtype)

    def stay(x):
        return pltpu.with_memory_space_constraint(x, pltpu.HBM)

    def route(k):
        return [(i, i ^ k) for i in range(n_seq)]

    sizes = (channels // 2, channels // 2) if channels % 32 == 0 else (channels,)
    chunks = len(sizes)
    tables = [jnp.asarray(t) for t in dft_tables(total, n_seq)]

    def prep(jobs, tables):
        size = channels // chunks
        outs = [pltpu.VMEM((4, size, seq_len), jnp.bfloat16)] * (2 * len(jobs))
        outs += [pltpu.VMEM(t.shape[1:] if i < 2 else t.shape, t.dtype) for i, t in enumerate(tables)]
        fields = [
            x.reshape(n_seq, chunks, size, seq_len) for x in (values, filter_taps, cotangent, gate_acts)
        ]
        ready = pl.pallas_call(
            functools.partial(prep_kernel, jobs, len(tables)),
            out_shape=outs,
            in_specs=[hbm] * (4 + len(tables)),
            out_specs=[vmem] * len(outs),
            scratch_shapes=[
                pltpu.VMEM((len(jobs), 3, 2, size, seq_len), jnp.bfloat16),
                pltpu.VMEM((len(jobs), 2, size, seq_len), jnp.float32),
                pltpu.SemaphoreType.DMA((len(jobs), 4)),
                pltpu.SemaphoreType.DMA((max(len(tables), 1),)),
            ],
            compiler_params=pltpu.CompilerParams(vmem_limit_bytes=8 * 2**20),
            cost_estimate=pl.CostEstimate(flops=0, bytes_accessed=4 * 2**20, transcendentals=0),
            name="prep",
        )(*(stay(x) for x in (*fields, *tables)))
        for at, (j, chunk) in enumerate(jobs):
            for low in range(2):
                sent[chunk, 2 * j + low] = ready[2 * at + low]
        return ready[2 * len(jobs) :]

    sent, got = {}, {}
    if chunks > 1 and n_seq > 2:
        jobs = [(j, chunk) for chunk in range(chunks) for j in reversed(range(n_seq // 2))]
        prep(jobs[: n_seq // 2 - 1], [])
        tables = prep(jobs[n_seq // 2 - 1 :], tables)
    else:
        fields = (values, filter_taps.astype(jnp.bfloat16), cotangent, gate_acts)
        tables[:2] = [t[me] for t in tables[:2]]
        for k in range(n_seq):
            rows_k = [lax.dynamic_slice_in_dim(x, (me ^ k) * channels, channels, 0) for x in fields]
            sent[0, k] = jnp.stack(rows_k)
    for chunk in range(chunks):
        for k in reversed(range(n_seq)):
            block = sent[chunk, k]
            got[chunk, k] = lax.ppermute(block, "seq", route(k)) if k else block

    places = list(range(outer))
    if tokens == LANES:
        for s, far, near in np.ndindex(n_seq, n_far, n_near):
            places[(s * n_far + far) * n_near + near] = (near * n_seq + s) * n_far + far
    grads, before, offset = None, [], 0
    for chunk, size in enumerate(sizes):
        last = chunk == chunks - 1
        args = [*(got[chunk, k] for k in range(n_seq)), *tables]
        specs = [vmem] * len(args)
        aliases = {}
        if chunk:
            aliases = {len(args): 0}
            args.append(grads)
            specs.append(hbm)
        group = size if size <= 24 else 8
        long = pltpu.VMEM(((size + 8) * (outer + PAD), LANES), jnp.float32)
        taps32 = pltpu.VMEM(((outer + 8) * (size + PAD), LANES), jnp.float32)
        grads, more = pl.pallas_call(
            functools.partial(mixer_kernel, n_seq, group, offset, places, last),
            out_shape=[
                pltpu.HBM((outer, 2 * channels, LANES), jnp.bfloat16),
                pltpu.VMEM((size * outer, 2 * LANES) if last else (n_seq, size, seq_len), jnp.float32),
            ],
            in_specs=specs,
            out_specs=[hbm, vmem],
            input_output_aliases=aliases,
            scratch_shapes=[long] * 4
            + [
                pltpu.VMEM(((outer + 8) * (2 * size + PAD), LANES), jnp.float32),
                pltpu.VMEM((2, outer, size, LANES), jnp.bfloat16),
                pltpu.SemaphoreType.DMA((2,)),
            ]
            + [taps32] * (not last),
            compiler_params=pltpu.CompilerParams(vmem_limit_bytes=24 * 2**20),
            cost_estimate=pl.CostEstimate(flops=5 * 10**9, bytes_accessed=2 * 2**20, transcendentals=0),
            name="mixer",
        )(*args)
        if not last:
            before.append(more)
        offset += size
    if tokens != LANES:
        grads = grads.reshape(outer, 2 * channels, LANES // tokens, tokens).transpose(0, 2, 1, 3)
        grads = grads.reshape(n_seq, n_far, n_near, 2 * channels, tokens).transpose(2, 0, 1, 3, 4)
        grads = grads.reshape(n_seq * n_chan, 2 * channels, tokens)
    spread = lax.all_to_all(grads, ("near", "seq", "far"), 0, 0, tiled=True)

    args = [more, *tables[3:], *before]
    taps_blocks = pl.pallas_call(
        functools.partial(lags_kernel, n_seq, group, size),
        out_shape=[jax.ShapeDtypeStruct((channels, seq_len), jnp.bfloat16)] * n_seq,
        in_specs=[vmem] * len(args),
        out_specs=[vmem] * n_seq,
        scratch_shapes=[taps32],
        compiler_params=pltpu.CompilerParams(vmem_limit_bytes=16 * 2**20),
        cost_estimate=pl.CostEstimate(flops=10**9, bytes_accessed=2**20, transcendentals=0),
        name="lags",
    )(*args)
    taps_got = [lax.ppermute(taps_blocks[k], "seq", route(k)) if k else taps_blocks[0] for k in range(n_seq)]
    taps_grad, w_held = pl.pallas_call(
        functools.partial(taps_kernel, n_seq),
        out_shape=[
            jax.ShapeDtypeStruct((n_seq, channels, seq_len), jnp.float32),
            pltpu.VMEM((w_value.shape[0] * (SLABS + KEPT) // SLABS, w_value.shape[1]), w_value.dtype),
        ],
        in_specs=[hbm] * 2 + [vmem] * n_seq,
        out_specs=[vmem] * 2,
        scratch_shapes=[pltpu.SemaphoreType.DMA((2,))],
        compiler_params=pltpu.CompilerParams(vmem_limit_bytes=8 * 2**20),
        name="taps",
    )(stay(w_value), stay(w_gate), *taps_got)

    held = jnp.bfloat16 if channels % 16 == 0 else jnp.float32
    args = [w_held, stay(w_gate), spread]
    input_grad = pl.pallas_call(
        functools.partial(project_kernel, n_seq, n_far, n_near, sizes),
        out_shape=jax.ShapeDtypeStruct((tokens, w_value.shape[0]), jnp.bfloat16),
        in_specs=[vmem, hbm, vmem],
        out_specs=vmem,
        scratch_shapes=[
            pltpu.VMEM((2, rows * n_chan, tokens), held),
            pltpu.VMEM((w_gate.shape[0] * (SLABS - KEPT) // SLABS, w_gate.shape[1]), w_gate.dtype),
            pltpu.VMEM((w_gate.shape[0], tokens), jnp.float32),
            pltpu.SemaphoreType.DMA,
        ],
        compiler_params=pltpu.CompilerParams(vmem_limit_bytes=16 * 2**20),
        name="project",
    )(*args)
    return input_grad, taps_grad.reshape(rows, seq_len)


def solution(mesh):
    n_seq, n_chan = mesh.shape["seq"], mesh.shape["chan"]
    n_far = math.gcd(n_chan, 4)
    parts = Mesh(mesh.devices.reshape(n_seq, n_far, n_chan // n_far), ("seq", "far", "near"))
    chan = ("far", "near")
    return jax.shard_map(
        functools.partial(local, n_seq, n_far, n_chan // n_far),
        mesh=parts,
        in_specs=(P(chan, "seq"), P(chan, "seq"), P(chan, "seq"), P(chan, "seq"), P(), P()),
        out_specs=(P(("seq", *chan), None), P(chan, "seq")),
        check_vma=False,
    )
```

```python
import functools
import math

import jax
import jax.numpy as jnp
import numpy as np
from jax import lax
from jax.experimental import pallas as pl
from jax.experimental.pallas import tpu as pltpu
from jax.sharding import Mesh
from jax.sharding import PartitionSpec as P

LANES = 128
VALUE, TAPS, COT, GATE = range(4)
SLABS = 8
KEPT = 3
PAD = 8


def halves(table):
    high = table.astype(jnp.bfloat16)
    low = (table - high.astype(np.float64)).astype(jnp.bfloat16)
    return high, low


def dft_tables(total, n_seq):
    outer = total // LANES
    k1 = np.arange(outer) + 0.25
    a = np.arange(outer)
    b = np.arange(LANES)
    first = np.exp(-2j * np.pi * np.outer(k1, a) / outer)
    first = np.concatenate([first.real, first.imag], 0)
    turn = np.exp(-2j * np.pi * np.outer(k1, b) / total)
    second = np.exp(-2j * np.pi * np.outer(b, b) / LANES)
    second = np.block([[second.real, second.imag], [-second.imag, second.real]])
    back_second = second.T / total / math.sqrt(total)
    back_first = np.exp(2j * np.pi * np.outer(a, k1) / outer)
    back_first = np.concatenate([back_first.real, -back_first.imag], 1)

    parts = first.reshape(2 * outer, n_seq, outer // n_seq)
    orders = np.arange(n_seq)[:, None] ^ np.arange(n_seq)
    first = np.stack([parts[:, order].reshape(2 * outer, outer) for order in orders])
    f_hi, f_lo = halves(first)
    s_hi, s_lo = halves(second)
    bs_hi, bs_lo = halves(back_second)
    bf_hi, bf_lo = halves(back_first)
    return (
        np.concatenate([f_hi, f_lo], 2),
        np.concatenate([f_hi, f_hi, f_lo], 2),
        np.concatenate([s_hi, s_hi, s_lo], 0),
        turn.real.astype(np.float32),
        turn.imag.astype(np.float32),
        np.concatenate([bs_hi, bs_hi, bs_lo], 0),
        np.concatenate([bf_hi, bf_hi, bf_lo], 1),
    )


def split_terms(x):
    high = x.astype(jnp.bfloat16)
    low = (x - high.astype(jnp.float32)).astype(jnp.bfloat16)
    return high, low


def dot(left, right):
    return jnp.dot(left, right, preferred_element_type=jnp.float32)


def wide_dot(x, table):
    high, low = split_terms(x)
    return dot(jnp.concatenate([high, low, high], 1), table)


def prep_kernel(jobs, n_tables, values, filter_taps, cotangent, gate_acts, *rest):
    tables, rest = rest[:n_tables], rest[n_tables:]
    (narrow, wide, sems, table_sems), rest = rest[-4:], rest[:-4]
    outs, held = rest[: 2 * len(jobs)], rest[2 * len(jobs) :]
    me = lax.axis_index("seq")
    copies = []
    for at, (j, chunk) in enumerate(jobs):
        both = pl.ds(lax.bitwise_xor(lax.shift_right_logical(me, 1), j) * 2, 2)
        copies.append([pltpu.make_async_copy(filter_taps.at[both, chunk], wide.at[at], sems.at[at, 3])])
        for i, ref in enumerate((values, cotangent, gate_acts)):
            copies[-1].append(pltpu.make_async_copy(ref.at[both, chunk], narrow.at[at, i], sems.at[at, i]))
        for copy in copies[-1]:
            copy.start()
    brought = [
        pltpu.make_async_copy(tables[i].at[me] if i < 2 else tables[i], held[i], table_sems.at[i])
        for i in range(n_tables)
    ]
    for copy in brought:
        copy.start()
    for at in range(len(jobs)):
        for copy in copies[at]:
            copy.wait()
        for low in range(2):
            side = lax.bitwise_xor(lax.bitwise_and(me, 1), low)
            out = outs[2 * at + low]
            out[TAPS] = wide[at, side].astype(jnp.bfloat16)
            for i, field in enumerate((VALUE, COT, GATE)):
                out[field] = narrow[at, i, side]
    for copy in brought:
        copy.wait()


def in_block(body):
    pl.when(lax.axis_index("seq") >= 0)(body)


def run_behind(tasks):
    tasks, live = list(tasks), []
    while tasks or live:
        live = [task for task in live if next(task, StopIteration) is None]
        if tasks:
            live.append(tasks.pop(0))
            next(live[-1])


def inverse(get, group, outer, turn, tables, put):
    (tr, ti), (bs3, bf3) = turn, tables
    high, low = split_terms(get())
    yield
    mid = dot(jnp.concatenate([high, low, high], 1), bs3[...])
    yield
    terms = []
    for pair in range(group // 2):
        cols = []
        for i in range(2):
            rows = slice((2 * pair + i) * outer, (2 * pair + i + 1) * outer)
            re, im = mid[rows, :LANES], mid[rows, LANES:]
            cols.append(jnp.concatenate([re * tr + im * ti, im * tr - re * ti], 0))
        terms.append(split_terms(jnp.concatenate(cols, 1)))
    yield
    ys = [dot(bf3[...], jnp.concatenate([high, low, high], 0)) for high, low in terms]
    yield
    for pair, y in enumerate(ys):
        for i in range(2):
            put(2 * pair + i, y[:, i * LANES : (i + 1) * LANES])
    yield


def taps_part(taps32, channels, source, part, own_outer):
    start = (source * own_outer + part) * (channels + PAD)
    start = pl.multiple_of(start, PAD) if channels % PAD == 0 else start
    return taps32[pl.ds(start, channels), :]


def mixer_kernel(n_seq, group, offset, places, last, *rest):
    blocks, rest = rest[:n_seq], rest[n_seq:]
    (f2, f3, s3, turn_re, turn_im, bs3, bf3), rest = rest[:7], rest[7:]
    if offset:
        rest = rest[1:]
    if last:
        grads, products, sig, taps, up, cot, grads32, grads16, sems = rest
    else:
        grads, taps_out, sig, taps, up, cot, grads32, grads16, sems, taps32 = rest
    me = lax.axis_index("seq")
    _, channels, seq_len = blocks[0].shape
    outer = grads.shape[0]
    pitch, wide, narrow = outer + PAD, 2 * channels + PAD, channels + PAD
    own_outer = seq_len // LANES

    def stage(field, ref):
        for k in range(n_seq):
            for part in range(own_outer):
                cols = pl.ds(part * LANES, LANES)
                x = blocks[k][field, :, cols].astype(jnp.float32)
                rows = pl.ds(k * own_outer + part, channels, stride=pitch)
                if field == COT:
                    source = lax.bitwise_xor(me, k)
                    cot[pl.ds(source * own_outer + part, channels, stride=pitch), :] = x
                    x = x * blocks[k][GATE, :, cols].astype(jnp.float32)
                ref[rows, :] = x

    tr, ti = turn_re[...], turn_im[...]

    def forward(ref, field, base, out):
        exact = field != COT
        if base == 0:
            stage(field, ref)
        yield
        turned = []
        ys = []
        for pair in range(group // 2):
            xs = [ref[pl.ds((base + 2 * pair + i) * pitch, outer), :] for i in range(2)]
            x = jnp.concatenate(xs, 1)
            if exact:
                high = x.astype(jnp.bfloat16)
                ys.append(dot(f2[...], jnp.concatenate([high, high], 0)))
            else:
                high, low = split_terms(x)
                ys.append(dot(f3[...], jnp.concatenate([high, low, high], 0)))
        yield
        for y in ys:
            for i in range(2):
                re = y[:outer, i * LANES : (i + 1) * LANES]
                im = y[outer:, i * LANES : (i + 1) * LANES]
                turned.append(jnp.concatenate([re * tr - im * ti, re * ti + im * tr], 1))
        high, low = split_terms(jnp.concatenate(turned, 0))
        yield
        spec = dot(jnp.concatenate([high, low, high], 1), s3[...])
        out += [spec[:, :LANES], spec[:, LANES:]]
        yield

    def times(left, right, conj):
        (ar, ai), (br, bi) = left, right
        if conj:
            return jnp.concatenate([ar * br + ai * bi, ai * br - ar * bi], 1)
        return jnp.concatenate([ar * br - ai * bi, ar * bi + ai * br], 1)

    def backward(left, right, conj, base, put):
        yield
        yield from inverse(
            lambda: times(left, right, conj), group, outer, (tr, ti), (bs3, bf3), lambda ch, y: put(base + ch, y)
        )

    def keep_product(left, right, base):
        products[pl.ds(base * outer, group * outer), :] = times(left, right, True)
        yield

    copies = []

    def send(side):
        rows = slice(side * channels, (side + 1) * channels)
        for a in range(outer):
            grads16[side, places[a]] = grads32[a * wide + rows.start : a * wide + rows.stop, :].astype(jnp.bfloat16)
        to = grads.at[:, pl.ds(2 * offset + side * channels, channels), :]
        copies.append(pltpu.make_async_copy(grads16.at[side], to, sems.at[side]))
        copies[-1].start()

    def put_gate(ch, y):
        held = cot[pl.ds(ch * pitch, outer), :]
        grads32[pl.ds(channels + ch, outer, stride=wide), :] = y * held
        if ch == channels - 1:
            send(1)

    def put_value(ch, y):
        grads32[pl.ds(ch, outer, stride=wide), :] = y
        if ch == channels - 1:
            send(0)

    def put_taps(ch, y):
        taps32[pl.ds(ch, outer, stride=narrow), :] = y

    tasks = []
    for base in range(0, channels, group):
        k, v, u = [], [], []
        tasks += [
            forward(taps, TAPS, base, k),
            forward(sig, VALUE, base, v),
            forward(up, COT, base, u),
            backward(k, v, False, base, put_gate),
            backward(u, k, True, base, put_value),
            keep_product(u, v, base) if last else backward(u, v, True, base, put_taps),
        ]
    run_behind(tasks)

    if not last:
        for k in range(n_seq):
            source = lax.bitwise_xor(me, k)
            for part in range(own_outer):
                taps_out[k, :, pl.ds(part * LANES, LANES)] = taps_part(taps32, channels, source, part, own_outer)
    for copy in copies:
        copy.wait()


def lags_kernel(n_seq, group, channels, products, turn_re, turn_im, bs3, bf3, *rest):
    outs, taps32 = rest[-n_seq - 1 : -1], rest[-1]
    before = rest[: -n_seq - 1]
    me = lax.axis_index("seq")
    outer = products.shape[0] // channels
    own_outer = outs[0].shape[1] // LANES

    def put(ch, y):
        taps32[pl.ds(ch, outer, stride=channels + PAD), :] = y

    turn = turn_re[...], turn_im[...]

    def task(base):
        rows = pl.ds(base * outer, group * outer)
        return inverse(
            lambda: products[rows, :], group, outer, turn, (bs3, bf3), lambda ch, y: put(base + ch, y)
        )

    run_behind(task(base) for base in range(0, channels, group))
    for k in range(n_seq):
        source = lax.bitwise_xor(me, k)
        for part in range(own_outer):
            cols = pl.ds(part * LANES, LANES)
            parts = [x[k, :, cols] for x in before] + [taps_part(taps32, channels, source, part, own_outer)]
            outs[k][:, cols] = jnp.concatenate(parts, 0).astype(jnp.bfloat16)


def taps_kernel(n_seq, w_value, w_gate, *rest):
    taps_in, (out, w_held, sems) = rest[:n_seq], rest[n_seq:]
    me = lax.axis_index("seq")
    rows = w_value.shape[0]
    keep = w_held.shape[0] - rows
    copies = [
        pltpu.make_async_copy(w_value, w_held.at[:rows, :], sems.at[0]),
        pltpu.make_async_copy(w_gate.at[:keep, :], w_held.at[rows:, :], sems.at[1]),
    ]
    for copy in copies:
        copy.start()
    for k in range(n_seq):
        out[lax.bitwise_xor(me, k)] = taps_in[k][...].astype(jnp.float32)
    for copy in copies:
        copy.wait()


def project_kernel(n_seq, n_far, n_near, sizes, w_held, w_gate, spread, out, held, gate_held, total, ready, sem, out_sems):
    features = w_gate.shape[0]
    split = features - gate_held.shape[0]
    copy = pltpu.make_async_copy(w_gate.at[split:, :], gate_held, sem)
    copy.start()
    middle = (split + features) // 2 // LANES * LANES
    pieces_out = [slice(0, split), slice(split, middle), slice(middle, features)]

    def leaving(i):
        at = pieces_out[i]
        return pltpu.make_async_copy(ready.at[:, at], out.at[:, at], out_sems.at[i])

    share = sum(sizes)
    firsts = [sum(sizes[:i]) for i in range(len(sizes))]

    def before():
        for source, (near, s, far) in enumerate(np.ndindex(n_near, n_seq, n_far)):
            block = spread[source].astype(jnp.float32)
            rows = pl.ds(((far * n_near + near) * n_seq + s) * share, share)
            for g in range(2):
                pieces = [block[2 * at + g * size : 2 * at + (g + 1) * size] for at, size in zip(firsts, sizes)]
                held[g, rows, :] = jnp.concatenate(pieces, 0).astype(held.dtype)
        values, gates = (held[g].astype(jnp.bfloat16) for g in range(2))
        total[...] = dot(w_held[:features, :], values)
        ready[:, :split] = (total[:split, :] + dot(w_held[features:, :], gates)).T.astype(jnp.bfloat16)
        leaving(0).start()

    in_block(before)
    copy.wait()
    gates = held[1].astype(jnp.bfloat16)
    for i in (1, 2):
        at = pieces_out[i]
        rest = dot(gate_held[at.start - split : at.stop - split, :], gates)
        ready[:, at] = (total[at, :] + rest).T.astype(jnp.bfloat16)
        leaving(i).start()
    for i in range(3):
        leaving(i).wait()


def local(n_seq, n_far, n_near, values, gate_acts, cotangent, filter_taps, w_value, w_gate):
    rows, seq_len = values.shape
    n_chan = n_far * n_near
    total = seq_len * n_seq
    channels = rows // n_seq
    outer = total // LANES
    tokens = total // (n_seq * n_chan)
    me = lax.axis_index("seq")
    vmem = pl.BlockSpec(memory_space=pltpu.VMEM)
    hbm = pl.BlockSpec(memory_space=pltpu.HBM)

    def like(x):
        return pltpu.VMEM(x.shape, x.dtype)

    def stay(x):
        return pltpu.with_memory_space_constraint(x, pltpu.HBM)

    def route(k):
        return [(i, i ^ k) for i in range(n_seq)]

    sizes = (channels // 2, channels // 2) if channels % 32 == 0 else (channels,)
    chunks = len(sizes)
    tables = [jnp.asarray(t) for t in dft_tables(total, n_seq)]

    def prep(jobs, tables):
        size = channels // chunks
        outs = [pltpu.VMEM((4, size, seq_len), jnp.bfloat16)] * (2 * len(jobs))
        outs += [pltpu.VMEM(t.shape[1:] if i < 2 else t.shape, t.dtype) for i, t in enumerate(tables)]
        fields = [
            x.reshape(n_seq, chunks, size, seq_len) for x in (values, filter_taps, cotangent, gate_acts)
        ]
        ready = pl.pallas_call(
            functools.partial(prep_kernel, jobs, len(tables)),
            out_shape=outs,
            in_specs=[hbm] * (4 + len(tables)),
            out_specs=[vmem] * len(outs),
            scratch_shapes=[
                pltpu.VMEM((len(jobs), 3, 2, size, seq_len), jnp.bfloat16),
                pltpu.VMEM((len(jobs), 2, size, seq_len), jnp.float32),
                pltpu.SemaphoreType.DMA((len(jobs), 4)),
                pltpu.SemaphoreType.DMA((max(len(tables), 1),)),
            ],
            compiler_params=pltpu.CompilerParams(vmem_limit_bytes=8 * 2**20),
            cost_estimate=pl.CostEstimate(flops=0, bytes_accessed=4 * 2**20, transcendentals=0),
            name="prep",
        )(*(stay(x) for x in (*fields, *tables)))
        for at, (j, chunk) in enumerate(jobs):
            for low in range(2):
                sent[chunk, 2 * j + low] = ready[2 * at + low]
        return ready[2 * len(jobs) :]

    sent, got = {}, {}
    if chunks > 1 and n_seq > 2:
        jobs = [(j, chunk) for chunk in range(chunks) for j in reversed(range(n_seq // 2))]
        prep(jobs[: n_seq // 2 - 1], [])
        tables = prep(jobs[n_seq // 2 - 1 :], tables)
    else:
        fields = (values, filter_taps.astype(jnp.bfloat16), cotangent, gate_acts)
        tables[:2] = [t[me] for t in tables[:2]]
        for k in range(n_seq):
            rows_k = [lax.dynamic_slice_in_dim(x, (me ^ k) * channels, channels, 0) for x in fields]
            sent[0, k] = jnp.stack(rows_k)
    for chunk in range(chunks):
        for k in reversed(range(n_seq)):
            block = sent[chunk, k]
            got[chunk, k] = lax.ppermute(block, "seq", route(k)) if k else block

    places = list(range(outer))
    if tokens == LANES:
        for s, far, near in np.ndindex(n_seq, n_far, n_near):
            places[(s * n_far + far) * n_near + near] = (near * n_seq + s) * n_far + far
    grads, before, offset = None, [], 0
    for chunk, size in enumerate(sizes):
        last = chunk == chunks - 1
        args = [*(got[chunk, k] for k in range(n_seq)), *tables]
        specs = [vmem] * len(args)
        aliases = {}
        if chunk:
            aliases = {len(args): 0}
            args.append(grads)
            specs.append(hbm)
        group = size if size <= 24 else 8
        long = pltpu.VMEM(((size + 8) * (outer + PAD), LANES), jnp.float32)
        taps32 = pltpu.VMEM(((outer + 8) * (size + PAD), LANES), jnp.float32)
        grads, more = pl.pallas_call(
            functools.partial(mixer_kernel, n_seq, group, offset, places, last),
            out_shape=[
                pltpu.HBM((outer, 2 * channels, LANES), jnp.bfloat16),
                pltpu.VMEM((size * outer, 2 * LANES) if last else (n_seq, size, seq_len), jnp.float32),
            ],
            in_specs=specs,
            out_specs=[hbm, vmem],
            input_output_aliases=aliases,
            scratch_shapes=[long] * 4
            + [
                pltpu.VMEM(((outer + 8) * (2 * size + PAD), LANES), jnp.float32),
                pltpu.VMEM((2, outer, size, LANES), jnp.bfloat16),
                pltpu.SemaphoreType.DMA((2,)),
            ]
            + [taps32] * (not last),
            compiler_params=pltpu.CompilerParams(vmem_limit_bytes=24 * 2**20),
            cost_estimate=pl.CostEstimate(flops=5 * 10**9, bytes_accessed=2 * 2**20, transcendentals=0),
            name="mixer",
        )(*args)
        if not last:
            before.append(more)
        offset += size
    if tokens != LANES:
        grads = grads.reshape(outer, 2 * channels, LANES // tokens, tokens).transpose(0, 2, 1, 3)
        grads = grads.reshape(n_seq, n_far, n_near, 2 * channels, tokens).transpose(2, 0, 1, 3, 4)
        grads = grads.reshape(n_seq * n_chan, 2 * channels, tokens)
    spread = lax.all_to_all(grads, ("near", "seq", "far"), 0, 0, tiled=True)

    args = [more, *tables[3:], *before]
    taps_blocks = pl.pallas_call(
        functools.partial(lags_kernel, n_seq, group, size),
        out_shape=[jax.ShapeDtypeStruct((channels, seq_len), jnp.bfloat16)] * n_seq,
        in_specs=[vmem] * len(args),
        out_specs=[vmem] * n_seq,
        scratch_shapes=[taps32],
        compiler_params=pltpu.CompilerParams(vmem_limit_bytes=16 * 2**20),
        cost_estimate=pl.CostEstimate(flops=10**9, bytes_accessed=2**20, transcendentals=0),
        name="lags",
    )(*args)
    taps_got = [lax.ppermute(taps_blocks[k], "seq", route(k)) if k else taps_blocks[0] for k in range(n_seq)]
    taps_grad, w_held = pl.pallas_call(
        functools.partial(taps_kernel, n_seq),
        out_shape=[
            jax.ShapeDtypeStruct((n_seq, channels, seq_len), jnp.float32),
            pltpu.VMEM((w_value.shape[0] * (SLABS + KEPT) // SLABS, w_value.shape[1]), w_value.dtype),
        ],
        in_specs=[hbm] * 2 + [vmem] * n_seq,
        out_specs=[vmem] * 2,
        scratch_shapes=[pltpu.SemaphoreType.DMA((2,))],
        compiler_params=pltpu.CompilerParams(vmem_limit_bytes=8 * 2**20),
        name="taps",
    )(stay(w_value), stay(w_gate), *taps_got)

    held = jnp.bfloat16 if channels % 16 == 0 else jnp.float32
    args = [w_held, stay(w_gate), spread]
    input_grad = pl.pallas_call(
        functools.partial(project_kernel, n_seq, n_far, n_near, sizes),
        out_shape=jax.ShapeDtypeStruct((tokens, w_value.shape[0]), jnp.bfloat16),
        in_specs=[vmem, hbm, vmem],
        out_specs=hbm,
        scratch_shapes=[
            pltpu.VMEM((2, rows * n_chan, tokens), held),
            pltpu.VMEM((w_gate.shape[0] * (SLABS - KEPT) // SLABS, w_gate.shape[1]), w_gate.dtype),
            pltpu.VMEM((w_gate.shape[0], tokens), jnp.float32),
            pltpu.VMEM((tokens, w_gate.shape[0]), jnp.bfloat16),
            pltpu.SemaphoreType.DMA,
            pltpu.SemaphoreType.DMA((3,)),
        ],
        compiler_params=pltpu.CompilerParams(vmem_limit_bytes=16 * 2**20),
        name="project",
    )(*args)
    return input_grad, taps_grad.reshape(rows, seq_len)


def solution(mesh):
    n_seq, n_chan = mesh.shape["seq"], mesh.shape["chan"]
    n_far = math.gcd(n_chan, 4)
    parts = Mesh(mesh.devices.reshape(n_seq, n_far, n_chan // n_far), ("seq", "far", "near"))
    chan = ("far", "near")
    return jax.shard_map(
        functools.partial(local, n_seq, n_far, n_chan // n_far),
        mesh=parts,
        in_specs=(P(chan, "seq"), P(chan, "seq"), P(chan, "seq"), P(chan, "seq"), P(), P()),
        out_specs=(P(("seq", *chan), None), P(chan, "seq")),
        check_vma=False,
    )
```
